512 devices in a mesh: blk: 128 (over x, y, z_hi, core), hid: 4 (over z_lo).
Axes of the slice: x: 4, y: 8, z: 8 (z_hi: 2, z_lo: 4; z = z_hi * 4 + z_lo), core: 2. Of those that a mesh axis runs over, the one named last changes fastest.
Arguments:
- out_grad: bfloat16 [16384, 2048], P('blk', 'hid'), may hold values from -6 to 6
- hidden: bfloat16 [16384, 8, 1536], P('blk', None, 'hid'), may hold values from -0.796875 to 0.796875
- gates: float32 [16384, 8], P('blk'), may hold values from 0.05 to 0.6
- expert_ids: int32 [16384, 8], P('blk'), may hold values from 0 to 127, all different within a row; in each aligned block of 128 rows (0 to 127, 128 to 255, ...) at most 12 rows name the same one
- down_weight: bfloat16 [128, 1536, 2048], P('blk', 'hid'), may hold values from -0.15625 to 0.15625
Outputs:
- weight_grad: bfloat16 [128, 1536, 2048], P('blk', 'hid')
- hidden_grad: bfloat16 [16384, 8, 1536], P('blk', None, 'hid')
- gate_grad: float32 [16384, 8], P('blk')
The draws below stay inside these ranges and needn't reach their ends.
Inputs may be any that keep to these rules, and one draw needn't show every extreme that they name: `expert_ids`: each row names 8 different experts; among the rows of one index of blk no expert is named more than 12 times, a bound that some block reaches.
All inputs are finite; a program needn't handle non-finite values.
Results may differ from the reference program's by a relative error of at most 0.0049.
Values may be sent and summed in bfloat16 or wider, within the bound.
A program may use at most 128 MiB of HBM per device.

```python
import math
import jax
import jax.numpy as jnp
import numpy as np
from jax import lax

D = 2048
F = 1536
TOPK = 8
TOK_DEV = 128
EXPERTS = 128
TOKENS = 16384
CAP = 12
N_BLK = 128


def level_of(stream_key, extent, pieces, low, top_value):
    factor_of = 1.0
    for position, parts in pieces:
        heights = jax.random.uniform(jax.random.fold_in(jax.random.fold_in(stream_key, 6), position), (parts,), jnp.float32, low / len(pieces), top_value / len(pieces))
        factor_of = factor_of * jnp.repeat(jnp.exp(heights), extent[position] // parts).reshape((-1,) + (1,) * (len(extent) - 1 - position))
    return factor_of


def assign_block(stream_key, own, number, rows, amount, top, limit, lean):
    sequence = jax.random.permutation(stream_key, amount)
    crowded, common = load_shares(amount, rows * top, limit, lean, True), load_shares(amount, rows * top, limit, lean, False)
    places = jnp.arange(amount)

    def named(lengths, turn):
        used = int((lengths > 0).sum())
        fixed = max(1, used // 4)
        moved = fixed + (places - fixed + turn * (used - fixed)) % max(1, amount - fixed)
        return jnp.zeros((amount,), jnp.int32).at[sequence[jnp.where(places < fixed, places, moved)]].set(jnp.asarray(lengths, jnp.int32))

    lengths = jnp.where(number % 4 == 0, named(crowded, number // 4), named(common, number - number // 4 - 1))
    mixed = jax.random.permutation(jax.random.fold_in(own, 3), amount)
    donor, receiver = mixed[0:amount // 2 * 2:2], mixed[1:amount // 2 * 2:2]
    margin = jnp.minimum(lengths[donor] - 1, limit - lengths[receiver]) // 2
    margin = jnp.where((donor == sequence[0]) | (receiver == sequence[0]) | (lengths[receiver] == 0), 0, jnp.maximum(margin, 0))
    moved = jax.random.randint(jax.random.fold_in(own, 4), (amount // 2,), 0, 1 << 20) % (margin + 1)
    lengths = lengths.at[donor].add(-moved).at[receiver].add(moved)
    labels = jnp.searchsorted(jnp.cumsum(lengths), jnp.arange(rows * top), side="right").astype(jnp.int32)
    listing = labels.reshape(top, rows).T
    listing = listing[jax.random.permutation(jax.random.fold_in(own, 1), rows)]
    turn = jax.random.randint(jax.random.fold_in(own, 2), (rows, 1), 0, top)
    return jnp.take_along_axis(listing, (jnp.arange(top)[None, :] + turn) % top, axis=1)


def load_shares(number_of, total, most, slope, full):
    weights = [(1 << 20) // math.isqrt(standing ** slope) + 1 for standing in range(1, number_of + 1)]
    largest = most if full else min(most, max(-(-total // number_of), total * weights[0] // sum(weights)))
    least = 1 if total - largest >= number_of - 1 else 0
    holding, rest = [largest] + [least] * (number_of - 1), total - largest - least * (number_of - 1)
    while rest > 0:
        free = [i for i in range(1, number_of) if holding[i] < largest] or [i for i in range(1, number_of) if holding[i] < most]
        pool, remaining = sum([weights[i] for i in free]), rest
        for i in free:
            more = min(most - holding[i], max(1, remaining * weights[i] // pool), rest)
            holding[i] = holding[i] + more
            rest = rest - more
    return np.array(holding)


def centred(stream_key, extent, scale, bound, split=(), held_as=jnp.bfloat16):
    result = scale * jax.random.normal(stream_key, extent, jnp.float32)
    if split:
        result = result * level_of(stream_key, extent, split, -0.22, 0.18)
    return jnp.clip(result, -bound, bound).astype(held_as)


def setup_inputs(seed: int = 0) -> dict:
    splits = jax.random.split(jax.random.key(seed), 6)
    out_grad = centred(splits[0], (TOKENS, D), 1.0, 6.0, ((0, 128), (1, 4)))
    hidden = centred(splits[1], (TOKENS, TOPK, F), 0.1, 0.796875, ((0, 128), (2, 4)))
    gates = jnp.clip(0.05 + 0.55 * jax.random.uniform(splits[2], (TOKENS, TOPK), jnp.float32) ** level_of(splits[2], (TOKENS, TOPK), ((0, 128),), -0.2, 0.2), 0.05, 0.6)
    expert_ids_keys = jax.random.split(jax.random.fold_in(splits[3], 1), TOKENS // TOK_DEV)
    expert_ids_turns = jax.random.permutation(jax.random.fold_in(splits[3], 3), TOKENS // TOK_DEV)
    expert_ids = jax.vmap(lambda own, number: assign_block(jax.random.fold_in(splits[3], 2), own, number, TOK_DEV, EXPERTS, TOPK, CAP, 2))(expert_ids_keys, expert_ids_turns).reshape((TOKENS, TOPK))
    down_weight = centred(splits[4], (EXPERTS, F, D), F ** -0.5, 0.15625, ((0, 128), (1, 4)))
    return dict(out_grad=out_grad, hidden=hidden, gates=gates, expert_ids=expert_ids, down_weight=down_weight)


def reference(out_grad, hidden, gates, expert_ids, down_weight):
    slot_count = TOKENS * TOPK
    row_limit = N_BLK * CAP
    weighted = (gates[:, :, None] * hidden.astype(jnp.float32)).astype(jnp.bfloat16)
    flat_weighted = weighted.reshape(slot_count, F)
    flat_ids = expert_ids.reshape(slot_count)
    order_slots = jnp.argsort(flat_ids, stable=True).astype(jnp.int32)
    counts = jax.ops.segment_sum(jnp.ones((slot_count,), jnp.int32), flat_ids, num_segments=EXPERTS)
    starts = (jnp.cumsum(counts) - counts).astype(jnp.int32)
    positions = jnp.arange(row_limit, dtype=jnp.int32)

    def one_expert(pre_all, inputs):
        weight, start_at, count_here = inputs
        filled = positions < count_here
        index = jnp.minimum(start_at + positions, slot_count - 1)
        slot_ids = order_slots[index]
        token_rows = slot_ids // TOPK
        expert_rows = jnp.where(filled[:, None], out_grad[token_rows], jnp.zeros((), jnp.bfloat16))
        hidden_rows = jnp.where(filled[:, None], flat_weighted[slot_ids], jnp.zeros((), jnp.bfloat16))
        pre_grad = jnp.dot(expert_rows, weight.T, preferred_element_type=jnp.float32).astype(jnp.bfloat16)
        grad_here = jnp.dot(hidden_rows.T, expert_rows, preferred_element_type=jnp.float32).astype(jnp.bfloat16)
        target = jnp.where(filled, slot_ids, slot_count)
        pre_all = pre_all.at[target].set(pre_grad, mode="drop")
        return pre_all, grad_here

    start_pre = jnp.zeros((slot_count, F), jnp.bfloat16)
    pre_all, weight_grad = lax.scan(one_expert, start_pre, (down_weight, starts, counts))
    pre_all = pre_all.reshape(TOKENS, TOPK, F).astype(jnp.float32)
    hidden_grad = (gates[:, :, None] * pre_all).astype(jnp.bfloat16)
    gate_grad = jnp.sum(hidden.astype(jnp.float32) * pre_all, axis=-1)
    return weight_grad, hidden_grad, gate_grad
```

```python
import functools

import jax
import jax.numpy as jnp
import numpy as np
from jax import lax
from jax.experimental import pallas as pl
from jax.experimental.pallas import tpu as pltpu
from jax.sharding import PartitionSpec as P

MESH = pl.DeviceIdType.MESH
BF = jnp.bfloat16
F32 = jnp.float32
NX, NY, NZ, NC = 4, 8, 8, 2
QUAD = 4
CAP = 12
GRP = QUAD * CAP
TOK = 128
LANE = 128
CHUNK = QUAD * TOK
CHUNK_ROWS = CHUNK + 4 * 8
COL = NY * GRP
NQ = NY * QUAD
UNITS = 384
FEATS = 2048
SLOTS = 1024


def dot(a, b):
    return jnp.dot(a, b, preferred_element_type=F32)


def dot_nt(a, b):
    return lax.dot_general(a, b, (((1,), (1,)), ((), ())), preferred_element_type=F32)


def dot_tn(a, b):
    return lax.dot_general(a, b, (((0,), (0,)), ((), ())), preferred_element_type=F32)


def kernel(
    og, ids16, weighted, hidden, tgt_row, tgt_col, perm, weight,
    slot_grads, gate_out, weight_grad,
    stage, ex, cols, gsel, sendx, recvx, rows,
    hs, hx, hq_send, hq, hrows,
    rq_send, rq, r2, rx, undo, w_vmem, wg_vmem, gate_recv,
    ex_s, ex_r, ra_s, ra_r, rb_s, rb_r, x_s, x_r,
    hx_s, hx_r, hq_s, hq_r, rq_s, rq_r, rx_s, rx_r, gt_s, gt_r, w_sem, o_sem,
):
    blk = lax.axis_index("blk")
    hid = lax.axis_index("hid")
    x = blk // 32
    y = (blk // 4) % 8
    zhi = (blk // 2) % 2
    core = blk % 2
    z = zhi * 4 + hid
    quad = zhi * 2 + core
    q = blk % 32

    def dev(x_, y_, z_, c_):
        return (x_ * 32 + y_ * 4 + (z_ // 4) * 2 + c_, z_ % 4)

    def dev_q(q_):
        return (x * 32 + q_, hid)

    def remote(src, dst, send_sem, recv_sem, device):
        copy = pltpu.make_async_remote_copy(
            src_ref=src, dst_ref=dst, send_sem=send_sem, recv_sem=recv_sem,
            device_id=device, device_id_type=MESH,
        )
        copy.start()

    def wait_for(ref, sem):
        pltpu.make_async_copy(ref, ref, sem).wait()

    pa = core * y + (1 - core) * z
    pb = core * z + (1 - core) * y

    def dev_ab(a, b):
        return dev(x, core * a + (1 - core) * b, core * b + (1 - core) * a, core)

    barrier = pltpu.get_barrier_semaphore()

    def greet(device):
        pl.semaphore_signal(barrier, inc=1, device_id=device, device_id_type=MESH)

    greeted = 0
    for step in (1, 7):
        greet(dev_ab((pa + step) % 8, pb))
        greet(dev_ab(pa, (pb + step) % 8))
        greeted += 2
    for d in range(1, 8):
        greet(dev((x + d // 2) % 4, y, z, (core + d % 2) % 2))
        greeted += 1
    for d in range(1, 4):
        greet((blk, (hid + d) % 4))
        greeted += 1

    def greet_q(d, c):
        greet(dev_q((q + d) % 32))
        return c

    lax.fori_loop(1, 32, greet_q, 0)
    greeted += 31

    def feature_block(c, z_):
        return (z_ % 4) * 512 + (z_ // 4) * 256 + c * 128

    for c in range(2):
        for z_ in range(8):
            pltpu.make_async_copy(
                weight.at[0, :, pl.ds(feature_block(c, z_), LANE)],
                w_vmem.at[:, pl.ds((c * 8 + z_) * LANE, LANE)],
                w_sem,
            ).start()

    for j in range(QUAD):
        stage[j, 0:TOK, :] = og[:, j * LANE:(j + 1) * LANE]
        stage[j, TOK:TOK + 16, :] = ids16[...]

    pl.semaphore_wait(barrier, greeted)

    for d in range(1, 4):
        other = (quad + d) % 4
        remote(
            stage.at[other], ex.at[quad], ex_s, ex_r.at[d],
            dev(x, y, (other // 2) * 4 + hid, other % 2),
        )
    ex[quad] = stage[quad]

    def select_hidden(dx):
        xd = (x + dx) % 4
        at = lax.broadcasted_iota(jnp.int32, (COL, SLOTS), 0) + xd * COL
        pick = jnp.where(at == tgt_row[...], 1.0, 0.0).astype(BF)
        picked = dot(pick, weighted[...]).astype(BF)
        if dx == 0:
            hx[x] = picked
        else:
            hs[dx] = picked
            remote(
                hs.at[dx], hx.at[x], hx_s, hx_r.at[dx],
                dev(xd, y, z, core),
            )

    for dx in (2, 1, 3, 0):
        select_hidden(dx)

    for d in range(1, 4):
        wait_for(ex.at[0], ex_r.at[d])
    own = cols.at[pb, pa]
    for j in range(QUAD):
        own[j * TOK:(j + 1) * TOK, :] = ex[j, 0:TOK, :]
    own[CHUNK:CHUNK_ROWS, :] = jnp.concatenate(
        [ex[j, TOK:TOK + 16, :].astype(F32)[0:8] for j in range(QUAD)], axis=0
    ).astype(BF)

    half_rows = CHUNK_ROWS // 2
    for step in range(1, 5):
        for way, sign in ((0, 1), (1, -1)):
            a = (pa - sign * (step - 1)) % 8
            if step > 1:
                wait_for(cols.at[0, 0], ra_r.at[way, step - 1])
            ref = cols.at[pb, a]
            if step == 4:
                ref = cols.at[pb, a, pl.ds(way * half_rows, half_rows)]
            remote(ref, ref, ra_s, ra_r.at[way, step], dev_ab((pa + sign) % 8, pb))
    for way in range(2):
        wait_for(cols.at[0, 0, pl.ds(0, half_rows)], ra_r.at[way, 4])

    def ring_wait(step):
        for way in range(2):
            for piece in range(2):
                if step < 4 or piece == way:
                    wait_for(cols.at[0, pl.ds(0, 4)], rb_r.at[way, step, piece])

    def ring_send(step):
        for way, sign in ((0, 1), (1, -1)):
            b = (pb - sign * (step - 1)) % 8
            for piece in range(2):
                if step > 1:
                    wait_for(cols.at[0, pl.ds(0, 4)], rb_r.at[way, step - 1, piece])
                if step < 4 or piece == way:
                    ref = cols.at[b, pl.ds(4 * piece, 4)]
                    remote(
                        ref, ref, rb_s, rb_r.at[way, step, piece],
                        dev_ab(pa, (pb + sign) % 8),
                    )

    before = jnp.where(
        lax.broadcasted_iota(jnp.int32, (TOK, TOK), 0)
        < lax.broadcasted_iota(jnp.int32, (TOK, TOK), 1), 1.0, 0.0,
    ).astype(BF)
    which = lax.broadcasted_iota(jnp.int32, (8, TOK), 0)
    wanted = (
        ((x + which // 2) % 4) * 32 + y * 4 + zhi * 2 + (core + which % 2) % 2
    ).astype(F32)

    def make_pick(col, a, b):
        ids = cols[b, a, CHUNK:CHUNK_ROWS, :].astype(F32)
        found = []
        for j in range(QUAD):
            hit = jnp.zeros((8, TOK), F32)
            for k in range(8):
                row = ids[j * 8 + k:j * 8 + k + 1, :]
                hit = hit + jnp.where(row == wanted, 1.0, 0.0)
            found.append(hit)
        rank = dot(jnp.concatenate(found, axis=0).astype(BF), before)
        code = jnp.concatenate(
            [
                jnp.where(found[j] > 0.5, rank[j * 8:(j + 1) * 8] + float(CAP * j), -1.0)
                for j in range(QUAD)
            ],
            axis=1,
        )
        at = lax.broadcasted_iota(jnp.int32, (GRP, CHUNK), 0).astype(F32)
        for e in range(8):
            gsel[col, e * GRP:(e + 1) * GRP, :] = jnp.where(
                at == code[e:e + 1, :], 1.0, 0.0
            ).astype(BF)

    def select(b, first):
        @pl.when(core == 0)
        def _():
            make_pick(b, 0, b)

        if first:
            @pl.when(core == 1)
            def _():
                def one(a, c):
                    make_pick(a, a, b)
                    return c

                lax.fori_loop(0, 8, one, 0)

        def one_chunk(a, c):
            col = core * a + (1 - core) * b
            out = dot(gsel[col], cols[b, a, 0:CHUNK, :]).astype(BF)
            place = pl.ds(pl.multiple_of(a * GRP, GRP), GRP)
            recvx[core, x, b, place, :] = out[0:GRP]
            for e in range(1, 8):
                sendx[b, e, place, :] = out[e * GRP:(e + 1) * GRP]
            return c

        lax.fori_loop(0, 8, one_chunk, 0)
        for e in (4, 5, 2, 3, 6, 7, 1):
            remote(
                sendx.at[b, e], recvx.at[core, x, b], x_s, x_r.at[e // 2],
                dev((x + e // 2) % 4, y, z, (core + e % 2) % 2),
            )

    ring_send(1)
    select(pb, True)
    ring_send(2)
    select((pb - 1) % 8, False)
    select((pb + 1) % 8, False)

    for dx in range(1, 4):
        wait_for(hx.at[0], hx_r.at[dx])
    swap = perm[...]

    def relay_hidden(g, c):
        block = jnp.concatenate(
            [hx[xs, pl.ds(pl.multiple_of(g * GRP, GRP), GRP), :] for xs in range(4)],
            axis=0,
        )
        out = dot(swap, block).astype(BF)
        for j in range(4):
            hq_send[g * 4 + j] = out[j * GRP:(j + 1) * GRP]
        return c

    lax.fori_loop(0, 8, relay_hidden, 0)
    hq[q] = hq_send[q]

    def send_hidden(d, c):
        qd = (q + d) % 32
        remote(hq_send.at[qd], hq.at[q], hq_s, hq_r, dev_q(qd))
        return c

    lax.fori_loop(1, 32, send_hidden, 0)

    ring_send(3)
    select((pb - 2) % 8, False)
    select((pb + 2) % 8, False)
    ring_send(4)
    select((pb - 3) % 8, False)
    select((pb + 3) % 8, False)
    ring_wait(4)
    select((pb + 4) % 8, False)

    wait_for(w_vmem, w_sem)
    for dx in (0, 1, 3, 2):
        xs = (x - dx) % 4
        if dx == 0:
            wait_for(recvx.at[0, 0], x_r.at[0])
        else:
            wait_for(recvx.at[:, 0], x_r.at[dx])
        place = pl.ds(pl.multiple_of(xs * COL, COL), COL)
        for a in range(8):
            rows[place, a * LANE:(a + 1) * LANE] = recvx[
                0, xs, :, a * GRP:(a + 1) * GRP, :
            ].reshape(COL, LANE)
            rows[place, FEATS // 2 + a * LANE:FEATS // 2 + (a + 1) * LANE] = recvx[
                1, xs, a
            ]
        hrows[place, :] = dot_nt(rows[place, :], w_vmem[...]).astype(BF)

    def return_group(i, c):
        ys = (y + 4 + i) % 8
        block = jnp.concatenate(
            [
                hrows[pl.ds(pl.multiple_of(xs * COL + ys * GRP, GRP), GRP), :]
                for xs in range(4)
            ],
            axis=0,
        )
        out = dot(swap, block).astype(BF)
        for j in range(4):
            rq_send[ys * 4 + j] = out[j * GRP:(j + 1) * GRP]
        for j in range(4):
            qd = ys * 4 + j

            @pl.when(qd != q)
            def _():
                remote(
                    rq_send.at[qd], rq.at[q], rq_s, rq_r.at[(ys - y) % 8], dev_q(qd)
                )

            @pl.when(qd == q)
            def _():
                rq[q] = rq_send[qd]
        return c

    lax.fori_loop(0, 8, return_group, 0)

    wait_for(hq.at[pl.ds(0, 31)], hq_r)

    def order_hidden(g, c):
        block = jnp.concatenate([hq[g * 4 + j] for j in range(4)], axis=0)
        out = dot(swap, block).astype(BF)
        for xs in range(4):
            hrows[pl.ds(pl.multiple_of(xs * COL + g * GRP, GRP), GRP), :] = out[
                xs * GRP:(xs + 1) * GRP
            ]
        return c

    lax.fori_loop(0, 8, order_hidden, 0)
    for c in range(2):
        for half in range(4):
            lanes = (c * 8 + half * 2) * LANE
            wg_vmem[:, lanes:lanes + 256] = dot_tn(
                hrows[...], rows[:, lanes:lanes + 256]
            ).astype(BF)
            for z_ in (half * 2, half * 2 + 1):
                pltpu.make_async_copy(
                    wg_vmem.at[:, pl.ds((c * 8 + z_) * LANE, LANE)],
                    weight_grad.at[0, :, pl.ds(feature_block(c, z_), LANE)],
                    o_sem,
                ).start()

    def relay_back(i, c):
        dy = (4 + i) % 8
        g = (y - dy) % 8

        @pl.when(dy == 0)
        def _():
            wait_for(rq.at[pl.ds(0, 3)], rq_r.at[dy])

        @pl.when(dy != 0)
        def _():
            wait_for(rq.at[pl.ds(0, 4)], rq_r.at[dy])

        block = jnp.concatenate([rq[g * 4 + j] for j in range(4)], axis=0)
        out = dot(swap, block).astype(BF)
        place = pl.ds(pl.multiple_of(g * GRP, GRP), GRP)
        for xs in range(4):
            r2[xs, place, :] = out[xs * GRP:(xs + 1) * GRP]
        rx[x, place, :] = r2[x, place, :]
        for dx in (2, 1, 3):
            xd = (x + dx) % 4
            remote(
                r2.at[xd, place], rx.at[x, place], rx_s, rx_r.at[dx],
                dev(xd, y, z, core),
            )
        return c

    lax.fori_loop(0, 8, relay_back, 0)

    def make_undo(i, c):
        place = pl.ds(pl.multiple_of(i * 128, 128), 128)
        at = lax.broadcasted_iota(jnp.int32, (128, NX * COL), 1)
        undo[place, :] = jnp.where(at == tgt_col[place, :], 1.0, 0.0).astype(BF)
        return c

    lax.fori_loop(0, 8, make_undo, 0)
    for dx in range(1, 4):
        wait_for(rx.at[0], rx_r.at[dx])
    ones = jnp.ones((8, LANE), BF)

    def take(i, c):
        place = pl.ds(pl.multiple_of(i * 256, 256), 256)
        grads = dot(undo[place, :], rx[...].reshape(NX * COL, UNITS))
        slot_grads[place, :] = grads.astype(BF)
        product = hidden[place, :].astype(F32) * grads
        total = product[:, 0:128] + product[:, 128:256] + product[:, 256:384]
        high = total.astype(BF)
        rest = total - high.astype(F32)
        middle = rest.astype(BF)
        low = (rest - middle.astype(F32)).astype(BF)
        gate_recv[hid, :, place] = (
            dot_nt(ones, high) + dot_nt(ones, middle) + dot_nt(ones, low)
        )
        return c

    lax.fori_loop(0, 4, take, 0)

    for d in range(1, 4):
        remote(
            gate_recv.at[hid], gate_recv.at[hid], gt_s, gt_r.at[d],
            (blk, (hid + d) % 4),
        )
    for d in range(1, 4):
        wait_for(gate_recv.at[0], gt_r.at[d])
    gate_out[...] = (gate_recv[0] + gate_recv[1]) + (gate_recv[2] + gate_recv[3])

    wait_for(stage.at[pl.ds(0, 3)], ex_s)
    wait_for(cols.at[0, pl.ds(0, 7)], ra_s)
    wait_for(cols.at[pl.ds(0, 7)], rb_s)
    wait_for(sendx.at[:, pl.ds(1, 7)], x_s)
    wait_for(hs.at[pl.ds(1, 3)], hx_s)
    wait_for(hq_send.at[pl.ds(0, 31)], hq_s)
    wait_for(rq_send.at[pl.ds(0, 31)], rq_s)
    wait_for(r2.at[pl.ds(0, 3)], rx_s)
    wait_for(gate_recv.at[pl.ds(0, 3)], gt_s)
    wait_for(wg_vmem, o_sem)


def fused(og, ids16, weighted, hidden, tgt_row, tgt_col, perm, weight):
    vmem = pl.BlockSpec(memory_space=pltpu.VMEM)
    hbm = pl.BlockSpec(memory_space=pl.ANY)
    dma = pltpu.SemaphoreType.DMA
    buf = lambda *shape: pltpu.VMEM(shape, BF)
    return pl.pallas_call(
        kernel,
        out_shape=(
            jax.ShapeDtypeStruct((SLOTS, UNITS), BF),
            jax.ShapeDtypeStruct((8, SLOTS), F32),
            jax.ShapeDtypeStruct((1, UNITS, FEATS), BF),
        ),
        in_specs=[vmem] * 7 + [hbm],
        out_specs=(vmem, vmem, hbm),
        scratch_shapes=[
            buf(QUAD, TOK + 16, LANE),
            buf(QUAD, TOK + 16, LANE),
            buf(8, 8, CHUNK_ROWS, LANE),
            buf(8, 8 * GRP, CHUNK),
            buf(8, 8, COL, LANE),
            buf(2, NX, 8, COL, LANE),
            buf(NX * COL, FEATS),
            buf(NX, COL, UNITS),
            buf(NX, COL, UNITS),
            buf(NQ, GRP, UNITS),
            buf(NQ, GRP, UNITS),
            buf(NX * COL, UNITS),
            buf(NQ, GRP, UNITS),
            buf(NQ, GRP, UNITS),
            buf(NX, COL, UNITS),
            buf(NX, COL, UNITS),
            buf(SLOTS, NX * COL),
            buf(UNITS, FEATS),
            buf(UNITS, FEATS),
            pltpu.VMEM((4, 8, SLOTS), F32),
            dma, dma((4,)),
            dma, dma((2, 5)),
            dma, dma((2, 5, 2)),
            dma, dma((4,)),
            dma, dma((4,)),
            dma, dma,
            dma, dma((8,)),
            dma, dma((4,)),
            dma, dma((4,)),
            dma, dma,
        ],
        compiler_params=pltpu.CompilerParams(
            collective_id=0, has_side_effects=True, vmem_limit_bytes=60 * 1024 * 1024
        ),
        cost_estimate=pl.CostEstimate(
            flops=20_000_000_000, bytes_accessed=8_000_000, transcendentals=0
        ),
    )(og, ids16, weighted, hidden, tgt_row, tgt_col, perm, weight)


def swap_matrix():
    at = np.arange(4 * GRP)
    outer, inner, row = at // GRP, at % GRP // CAP, at % CAP
    matrix = np.zeros((4 * GRP, 4 * GRP), np.float32)
    matrix[at, inner * GRP + outer * CAP + row] = 1.0
    return matrix


def shards(out_grad, hidden, gates, expert_ids, down_weight):
    onehot = (
        expert_ids[:, :, None] == jnp.arange(128, dtype=jnp.int32)[None, None, :]
    ).astype(F32)
    named = jnp.sum(onehot, axis=1)
    before = jnp.asarray(np.tril(np.ones((TOK, TOK), np.float32), -1), BF)
    count = dot(before, named.astype(BF))
    rank = jnp.sum(onehot * count[:, None, :], axis=2).astype(jnp.int32)
    target = expert_ids * CAP + rank
    weighted = (gates[:, :, None] * hidden.astype(F32)).astype(BF)
    ids16 = jnp.concatenate(
        [expert_ids.T.astype(BF), jnp.zeros((8, TOK), BF)], axis=0
    )
    slot_grads, gate_grad, weight_grad = fused(
        out_grad,
        ids16,
        weighted.reshape(SLOTS, UNITS),
        hidden.reshape(SLOTS, UNITS),
        target.reshape(1, SLOTS),
        target.reshape(SLOTS, 1),
        jnp.asarray(swap_matrix(), BF),
        down_weight,
    )
    slot_grads = slot_grads.reshape(TOK, 8, UNITS).astype(F32)
    hidden_grad = (gates[:, :, None] * slot_grads).astype(BF)
    return weight_grad, hidden_grad, gate_grad[0].reshape(TOK, 8)


def solution(mesh):
    placed = (
        P("blk", "hid"),
        P("blk", None, "hid"),
        P("blk", None),
        P("blk", None),
        P("blk", "hid", None),
    )
    return jax.shard_map(
        shards,
        mesh=mesh,
        in_specs=placed,
        out_specs=(P("blk", "hid", None), P("blk", None, "hid"), P("blk", None)),
        check_vma=False,
    )
```

```python
import jax
import jax.numpy as jnp
from jax import lax
from jax.experimental import pallas as pl
from jax.experimental.pallas import tpu as pltpu
from jax.sharding import PartitionSpec as P

MESH = pl.DeviceIdType.MESH
BF = jnp.bfloat16
F32 = jnp.float32
NX, NY, NZ, NC = 4, 8, 8, 2
QUAD = 4
CAP = 12
GRP = QUAD * CAP
TOK = 128
LANE = 128
CHUNK = QUAD * TOK
CHUNK_ROWS = CHUNK + 4 * 8
COL = NY * GRP
NQ = NY * QUAD
UNITS = 384
FEATS = 2048
SLOTS = 1024


def dot(a, b):
    return jnp.dot(a, b, preferred_element_type=F32)


def dot_nt(a, b):
    return lax.dot_general(a, b, (((1,), (1,)), ((), ())), preferred_element_type=F32)


def dot_tn(a, b):
    return lax.dot_general(a, b, (((0,), (0,)), ((), ())), preferred_element_type=F32)


def thirds(value):
    high = value.astype(BF)
    rest = value - high.astype(F32)
    middle = rest.astype(BF)
    return high, middle, (rest - middle.astype(F32)).astype(BF)


def kernel(
    og, hidden, gates, ids, weight,
    hidden_grad, gate_out, weight_grad,
    weighted, slot_target, slot_gate, stage, ex, cols, gsel, sendx, recvx, rows,
    hs, hx, hq_send, hq, hrows,
    rq_send, rq, r2, rx, undo, w_vmem, wg_vmem, gate_row, gate_recv,
    ex_s, ex_r, ra_s, ra_r, rb_s, rb_r, x_s, x_r,
    hx_s, hx_r, hq_s, hq_r, rq_s, rq_r, rx_s, rx_r, gt_s, gt_r, w_sem, o_sem,
):
    blk = lax.axis_index("blk")
    hid = lax.axis_index("hid")
    x = blk // 32
    y = (blk // 4) % 8
    zhi = (blk // 2) % 2
    core = blk % 2
    z = zhi * 4 + hid
    quad = zhi * 2 + core
    q = blk % 32

    def dev(x_, y_, z_, c_):
        return (x_ * 32 + y_ * 4 + (z_ // 4) * 2 + c_, z_ % 4)

    def dev_q(q_):
        return (x * 32 + q_, hid)

    def remote(src, dst, send_sem, recv_sem, device):
        copy = pltpu.make_async_remote_copy(
            src_ref=src, dst_ref=dst, send_sem=send_sem, recv_sem=recv_sem,
            device_id=device, device_id_type=MESH,
        )
        copy.start()

    def wait_for(ref, sem):
        pltpu.make_async_copy(ref, ref, sem).wait()

    pa = core * y + (1 - core) * z
    pb = core * z + (1 - core) * y

    def dev_ab(a, b):
        return dev(x, core * a + (1 - core) * b, core * b + (1 - core) * a, core)

    barrier = pltpu.get_barrier_semaphore()

    def greet(device):
        pl.semaphore_signal(barrier, inc=1, device_id=device, device_id_type=MESH)

    greeted = 0
    for step in (1, 7):
        greet(dev_ab((pa + step) % 8, pb))
        greet(dev_ab(pa, (pb + step) % 8))
        greeted += 2
    for d in range(1, 8):
        greet(dev((x + d // 2) % 4, y, z, (core + d % 2) % 2))
        greeted += 1
    for d in range(1, 4):
        greet((blk, (hid + d) % 4))
        greeted += 1

    def greet_q(d, c):
        greet(dev_q((q + d) % 32))
        return c

    lax.fori_loop(1, 32, greet_q, 0)
    greeted += 31

    def feature_block(c, z_):
        return (z_ % 4) * 512 + (z_ // 4) * 256 + c * 128

    for c in range(2):
        for z_ in range(8):
            pltpu.make_async_copy(
                weight.at[0, :, pl.ds(feature_block(c, z_), LANE)],
                w_vmem.at[:, pl.ds((c * 8 + z_) * LANE, LANE)],
                w_sem,
            ).start()

    lane = lax.broadcasted_iota(jnp.int32, (TOK, LANE), 1)
    own_ids = ids[...].astype(F32)
    both = jnp.concatenate(
        [own_ids, gates[...], jnp.zeros((TOK - 16, LANE), F32)], axis=0
    ).T
    id_lanes = jnp.where(lane < 8, both, 0.0)
    gate_lanes = jnp.zeros((TOK, LANE), F32)
    named = jnp.zeros((TOK, LANE), F32)
    for k in range(8):
        gate_lanes = jnp.where(lane % 8 == k, both[:, 8 + k:9 + k], gate_lanes)
        named = named + jnp.where(lane.astype(F32) == both[:, k:k + 1], 1.0, 0.0)
    ids16 = jnp.concatenate([own_ids, jnp.zeros((8, TOK), F32)], axis=0).astype(BF)
    for j in range(QUAD):
        stage[j, 0:TOK, :] = og[:, j * LANE:(j + 1) * LANE]
        stage[j, TOK:TOK + 16, :] = ids16

    high, middle, low = (part.astype(F32) for part in thirds(gate_lanes))
    mixed = jnp.where(
        lane < 8, high,
        jnp.where(lane < 16, middle, jnp.where(lane < 24, low, 0.0)),
    )
    earlier = jnp.where(
        lax.broadcasted_iota(jnp.int32, (TOK, TOK), 1)
        < lax.broadcasted_iota(jnp.int32, (TOK, TOK), 0), 1.0, 0.0,
    ).astype(BF)
    count = dot(earlier, named.astype(BF)).astype(BF)
    slot = lax.broadcasted_iota(jnp.int32, (SLOTS, LANE), 0)
    slot_lane = lax.broadcasted_iota(jnp.int32, (SLOTS, LANE), 1)
    token_of = jnp.where(slot // 8 == slot_lane, 1.0, 0.0).astype(BF)
    turn = slot % 8 == slot_lane % 8
    slot_gate[...] = jnp.broadcast_to(
        jnp.sum(
            jnp.where(turn, dot(token_of, mixed.astype(BF)), 0.0), axis=1, keepdims=True
        ),
        (SLOTS, LANE),
    )
    slot_id = jnp.sum(
        jnp.where(turn, dot(token_of, id_lanes.astype(BF)), 0.0), axis=1, keepdims=True
    )
    slot_rank = jnp.sum(
        jnp.where(slot_lane.astype(F32) == slot_id, dot(token_of, count), 0.0),
        axis=1, keepdims=True,
    )
    slot_target[...] = jnp.broadcast_to(slot_id * float(CAP) + slot_rank, (SLOTS, LANE))
    both = jnp.where(
        slot_lane == 0, slot_id, jnp.where(slot_lane == 1, slot_rank, 0.0)
    ).astype(BF)
    lane16 = lax.broadcasted_iota(jnp.int32, (16, LANE), 1)
    tgt_row = dot_nt(
        jnp.where(lane16 == 0, float(CAP), jnp.where(lane16 == 1, 1.0, 0.0)).astype(BF),
        both,
    )[0:1]
    for i in range(4):
        part = slice(i * 256, (i + 1) * 256)
        for j in range(3):
            weighted[part, j * LANE:(j + 1) * LANE] = (
                slot_gate[part, :] * hidden[part, j * LANE:(j + 1) * LANE].astype(F32)
            ).astype(BF)

    def select_hidden(dx):
        xd = (x + dx) % 4
        at = lax.broadcasted_iota(jnp.int32, (COL, SLOTS), 0) + xd * COL
        pick = jnp.where(at.astype(F32) == tgt_row, 1.0, 0.0).astype(BF)
        picked = dot(pick, weighted[...]).astype(BF)
        if dx == 0:
            hx[x] = picked
        else:
            hs[dx] = picked

    def send_hidden_x(dx):
        remote(
            hs.at[dx], hx.at[x], hx_s, hx_r.at[dx], dev((x + dx) % 4, y, z, core)
        )

    select_hidden(2)
    pl.semaphore_wait(barrier, greeted)

    for d in range(1, 4):
        other = (quad + d) % 4
        remote(
            stage.at[other], ex.at[quad], ex_s, ex_r.at[d],
            dev(x, y, (other // 2) * 4 + hid, other % 2),
        )
    ex[quad] = stage[quad]

    send_hidden_x(2)
    select_hidden(1)
    send_hidden_x(1)

    for d in range(1, 4):
        wait_for(ex.at[0], ex_r.at[d])
    own = cols.at[pb, pa]
    for j in range(QUAD):
        own[j * TOK:(j + 1) * TOK, :] = ex[j, 0:TOK, :]
    own[CHUNK:CHUNK_ROWS, :] = jnp.concatenate(
        [ex[j, TOK:TOK + 16, :].astype(F32)[0:8] for j in range(QUAD)], axis=0
    ).astype(BF)

    half_rows = CHUNK_ROWS // 2
    for step in range(1, 5):
        for way, sign in ((0, 1), (1, -1)):
            a = (pa - sign * (step - 1)) % 8
            if step > 1:
                wait_for(cols.at[0, 0], ra_r.at[way, step - 1])
            ref = cols.at[pb, a]
            if step == 4:
                ref = cols.at[pb, a, pl.ds(way * half_rows, half_rows)]
            remote(ref, ref, ra_s, ra_r.at[way, step], dev_ab((pa + sign) % 8, pb))
        if step == 1:
            select_hidden(3)
            send_hidden_x(3)
        if step == 2:
            select_hidden(0)
    for way in range(2):
        wait_for(cols.at[0, 0, pl.ds(0, half_rows)], ra_r.at[way, 4])

    def ring_has(step, way, piece):
        return step < 4 or piece // 2 == way

    def ring_wait(step):
        for piece in range(4):
            for way in range(2):
                if ring_has(step, way, piece):
                    wait_for(cols.at[0, pl.ds(0, 2)], rb_r.at[way, step, piece])

    def ring_send(step):
        for piece in range(4):
            for way, sign in ((0, 1), (1, -1)):
                b = (pb - sign * (step - 1)) % 8
                if step > 1:
                    wait_for(cols.at[0, pl.ds(0, 2)], rb_r.at[way, step - 1, piece])
                if ring_has(step, way, piece):
                    ref = cols.at[b, pl.ds(2 * piece, 2)]
                    remote(
                        ref, ref, rb_s, rb_r.at[way, step, piece],
                        dev_ab(pa, (pb + sign) % 8),
                    )

    before = jnp.where(
        lax.broadcasted_iota(jnp.int32, (TOK, TOK), 0)
        < lax.broadcasted_iota(jnp.int32, (TOK, TOK), 1), 1.0, 0.0,
    ).astype(BF)
    which = lax.broadcasted_iota(jnp.int32, (8, TOK), 0)
    wanted = (
        ((x + which // 2) % 4) * 32 + y * 4 + zhi * 2 + (core + which % 2) % 2
    ).astype(F32)

    def make_pick(col, a, b):
        ids = cols[b, a, CHUNK:CHUNK_ROWS, :].astype(F32)
        found = []
        for j in range(QUAD):
            hit = jnp.zeros((8, TOK), F32)
            for k in range(8):
                row = ids[j * 8 + k:j * 8 + k + 1, :]
                hit = hit + jnp.where(row == wanted, 1.0, 0.0)
            found.append(hit)
        rank = dot(jnp.concatenate(found, axis=0).astype(BF), before)
        code = jnp.concatenate(
            [
                jnp.where(found[j] > 0.5, rank[j * 8:(j + 1) * 8] + float(CAP * j), -1.0)
                for j in range(QUAD)
            ],
            axis=1,
        )
        at = lax.broadcasted_iota(jnp.int32, (GRP, CHUNK), 0).astype(F32)
        for e in range(8):
            gsel[col, e * GRP:(e + 1) * GRP, :] = jnp.where(
                at == code[e:e + 1, :], 1.0, 0.0
            ).astype(BF)

    def select(b, first):
        @pl.when(core == 0)
        def _():
            make_pick(b, 0, b)

        if first:
            @pl.when(core == 1)
            def _():
                def one(a, c):
                    make_pick(a, a, b)
                    return c

                lax.fori_loop(0, 8, one, 0)

        def one_chunk(a, c):
            col = core * a + (1 - core) * b
            out = dot(gsel[col], cols[b, a, 0:CHUNK, :]).astype(BF)
            place = pl.ds(pl.multiple_of(a * GRP, GRP), GRP)
            recvx[core, x, b, place, :] = out[0:GRP]
            for e in range(1, 8):
                sendx[b, e, place, :] = out[e * GRP:(e + 1) * GRP]
            return c

        lax.fori_loop(0, 8, one_chunk, 0)
        for e in (4, 5, 2, 3, 6, 7, 1):
            remote(
                sendx.at[b, e], recvx.at[core, x, b], x_s, x_r.at[e // 2],
                dev((x + e // 2) % 4, y, z, (core + e % 2) % 2),
            )

    ring_send(1)
    select(pb, True)
    ring_send(2)
    select((pb - 1) % 8, False)
    select((pb + 1) % 8, False)

    ring_send(3)
    select((pb - 2) % 8, False)
    select((pb + 2) % 8, False)
    ring_send(4)
    select((pb - 3) % 8, False)
    select((pb + 3) % 8, False)

    for dx in range(1, 4):
        wait_for(hx.at[0], hx_r.at[dx])
    out_row = lax.broadcasted_iota(jnp.int32, (4 * GRP, 4 * GRP), 0)
    outer = sum(jnp.where(out_row >= n * GRP, 1, 0) for n in range(1, 4))
    within = out_row - outer * GRP
    inner = sum(jnp.where(within >= n * CAP, 1, 0) for n in range(1, 4))
    from_row = inner * GRP + outer * CAP + within - inner * CAP
    in_row = lax.broadcasted_iota(jnp.int32, (4 * GRP, 4 * GRP), 1)
    swap = jnp.where(in_row == from_row, 1.0, 0.0).astype(BF)

    def relay_hidden(g, c):
        block = jnp.concatenate(
            [hx[xs, pl.ds(pl.multiple_of(g * GRP, GRP), GRP), :] for xs in range(4)],
            axis=0,
        )
        out = dot(swap, block).astype(BF)
        for j in range(4):
            hq_send[g * 4 + j] = out[j * GRP:(j + 1) * GRP]
        return c

    lax.fori_loop(0, 8, relay_hidden, 0)
    hq[q] = hq_send[q]

    def send_hidden(d, c):
        qd = (q + d) % 32
        remote(hq_send.at[qd], hq.at[q], hq_s, hq_r, dev_q(qd))
        return c

    lax.fori_loop(1, 32, send_hidden, 0)

    ring_wait(4)
    select((pb + 4) % 8, False)

    wait_for(w_vmem, w_sem)
    for dx in (0, 1, 3, 2):
        xs = (x - dx) % 4
        if dx == 0:
            wait_for(recvx.at[0, 0], x_r.at[0])
        else:
            wait_for(recvx.at[:, 0], x_r.at[dx])
        place = pl.ds(pl.multiple_of(xs * COL, COL), COL)
        for a in range(8):
            rows[place, a * LANE:(a + 1) * LANE] = recvx[
                0, xs, :, a * GRP:(a + 1) * GRP, :
            ].reshape(COL, LANE)
            rows[place, FEATS // 2 + a * LANE:FEATS // 2 + (a + 1) * LANE] = recvx[
                1, xs, a
            ]
        hrows[place, :] = dot_nt(rows[place, :], w_vmem[...]).astype(BF)

    def return_group(i, c):
        ys = (y + 4 + i) % 8
        block = jnp.concatenate(
            [
                hrows[pl.ds(pl.multiple_of(xs * COL + ys * GRP, GRP), GRP), :]
                for xs in range(4)
            ],
            axis=0,
        )
        out = dot(swap, block).astype(BF)
        for j in range(4):
            rq_send[ys * 4 + j] = out[j * GRP:(j + 1) * GRP]
        for j in range(4):
            qd = ys * 4 + j

            @pl.when(qd != q)
            def _():
                remote(
                    rq_send.at[qd], rq.at[q], rq_s, rq_r.at[(ys - y) % 8], dev_q(qd)
                )

            @pl.when(qd == q)
            def _():
                rq[q] = rq_send[qd]
        return c

    lax.fori_loop(0, 8, return_group, 0)

    wait_for(hq.at[pl.ds(0, 31)], hq_r)

    def order_hidden(g, c):
        block = jnp.concatenate([hq[g * 4 + j] for j in range(4)], axis=0)
        out = dot(swap, block).astype(BF)
        for xs in range(4):
            hrows[pl.ds(pl.multiple_of(xs * COL + g * GRP, GRP), GRP), :] = out[
                xs * GRP:(xs + 1) * GRP
            ]
        return c

    lax.fori_loop(0, 8, order_hidden, 0)
    for c in range(2):
        for half in range(4):
            lanes = (c * 8 + half * 2) * LANE
            wg_vmem[:, lanes:lanes + 256] = dot_tn(
                hrows[...], rows[:, lanes:lanes + 256]
            ).astype(BF)
            for z_ in (half * 2, half * 2 + 1):
                pltpu.make_async_copy(
                    wg_vmem.at[:, pl.ds((c * 8 + z_) * LANE, LANE)],
                    weight_grad.at[0, :, pl.ds(feature_block(c, z_), LANE)],
                    o_sem,
                ).start()

    def relay_back(i, c):
        dy = (4 + i) % 8
        g = (y - dy) % 8

        @pl.when(dy == 0)
        def _():
            wait_for(rq.at[pl.ds(0, 3)], rq_r.at[dy])

        @pl.when(dy != 0)
        def _():
            wait_for(rq.at[pl.ds(0, 4)], rq_r.at[dy])

        block = jnp.concatenate([rq[g * 4 + j] for j in range(4)], axis=0)
        out = dot(swap, block).astype(BF)
        place = pl.ds(pl.multiple_of(g * GRP, GRP), GRP)
        for xs in range(4):
            r2[xs, place, :] = out[xs * GRP:(xs + 1) * GRP]
        rx[x, place, :] = r2[x, place, :]
        for dx in (2, 1, 3):
            xd = (x + dx) % 4
            remote(
                r2.at[xd, place], rx.at[x, place], rx_s, rx_r.at[dx],
                dev(xd, y, z, core),
            )
        return c

    lax.fori_loop(0, 8, relay_back, 0)

    def make_undo(i, c):
        place = pl.ds(pl.multiple_of(i * 128, 128), 128)
        for j in range(NX * COL // LANE):
            at = lax.broadcasted_iota(jnp.int32, (128, LANE), 1) + j * LANE
            undo[place, j * LANE:(j + 1) * LANE] = jnp.where(
                at.astype(F32) == slot_target[place, :], 1.0, 0.0
            ).astype(BF)
        return c

    lax.fori_loop(0, 8, make_undo, 0)
    for dx in range(1, 4):
        wait_for(rx.at[0], rx_r.at[dx])
    ones = jnp.ones((8, LANE), BF)

    def take(i, c):
        place = pl.ds(pl.multiple_of(i * 256, 256), 256)
        grads = dot(undo[place, :], rx[...].reshape(NX * COL, UNITS))
        for j in range(3):
            part = slice(j * LANE, (j + 1) * LANE)
            hidden_grad[place, part] = (slot_gate[place, :] * grads[:, part]).astype(BF)
        product = hidden[place, :].astype(F32) * grads
        total = product[:, 0:128] + product[:, 128:256] + product[:, 256:384]
        gate_row[:, place] = sum(dot_nt(ones, part) for part in thirds(total))
        return c

    lax.fori_loop(0, 4, take, 0)
    in_turn = (
        lax.broadcasted_iota(jnp.int32, (8, SLOTS), 1) % 8
        == lax.broadcasted_iota(jnp.int32, (8, SLOTS), 0)
    )
    token_of = jnp.where(slot // 8 == slot_lane, 1.0, 0.0).astype(BF)
    gate_recv[hid] = sum(
        dot(part, token_of) for part in thirds(jnp.where(in_turn, gate_row[...], 0.0))
    )

    for d in range(1, 4):
        remote(
            gate_recv.at[hid], gate_recv.at[hid], gt_s, gt_r.at[d],
            (blk, (hid + d) % 4),
        )
    for d in range(1, 4):
        wait_for(gate_recv.at[0], gt_r.at[d])
    gate_out[...] = (gate_recv[0] + gate_recv[1]) + (gate_recv[2] + gate_recv[3])

    wait_for(stage.at[pl.ds(0, 3)], ex_s)
    wait_for(cols.at[0, pl.ds(0, 7)], ra_s)
    wait_for(cols.at[pl.ds(0, 7)], rb_s)
    wait_for(sendx.at[:, pl.ds(1, 7)], x_s)
    wait_for(hs.at[pl.ds(1, 3)], hx_s)
    wait_for(hq_send.at[pl.ds(0, 31)], hq_s)
    wait_for(rq_send.at[pl.ds(0, 31)], rq_s)
    wait_for(r2.at[pl.ds(0, 3)], rx_s)
    wait_for(gate_recv.at[pl.ds(0, 3)], gt_s)
    wait_for(wg_vmem, o_sem)


def fused(og, hidden, gates, ids, weight):
    vmem = pl.BlockSpec(memory_space=pltpu.VMEM)
    hbm = pl.BlockSpec(memory_space=pl.ANY)
    dma = pltpu.SemaphoreType.DMA
    buf = lambda *shape: pltpu.VMEM(shape, BF)
    return pl.pallas_call(
        kernel,
        out_shape=(
            jax.ShapeDtypeStruct((SLOTS, UNITS), BF),
            jax.ShapeDtypeStruct((8, TOK), F32),
            jax.ShapeDtypeStruct((1, UNITS, FEATS), BF),
        ),
        in_specs=[vmem] * 4 + [hbm],
        out_specs=(vmem, vmem, hbm),
        scratch_shapes=[
            buf(SLOTS, UNITS),
            pltpu.VMEM((SLOTS, LANE), F32),
            pltpu.VMEM((SLOTS, LANE), F32),
            buf(QUAD, TOK + 16, LANE),
            buf(QUAD, TOK + 16, LANE),
            buf(8, 8, CHUNK_ROWS, LANE),
            buf(8, 8 * GRP, CHUNK),
            buf(8, 8, COL, LANE),
            buf(2, NX, 8, COL, LANE),
            buf(NX * COL, FEATS),
            buf(NX, COL, UNITS),
            buf(NX, COL, UNITS),
            buf(NQ, GRP, UNITS),
            buf(NQ, GRP, UNITS),
            buf(NX * COL, UNITS),
            buf(NQ, GRP, UNITS),
            buf(NQ, GRP, UNITS),
            buf(NX, COL, UNITS),
            buf(NX, COL, UNITS),
            buf(SLOTS, NX * COL),
            buf(UNITS, FEATS),
            buf(UNITS, FEATS),
            pltpu.VMEM((8, SLOTS), F32),
            pltpu.VMEM((4, 8, TOK), F32),
            dma, dma((4,)),
            dma, dma((2, 5)),
            dma, dma((2, 5, 4)),
            dma, dma((4,)),
            dma, dma((4,)),
            dma, dma,
            dma, dma((8,)),
            dma, dma((4,)),
            dma, dma((4,)),
            dma, dma,
        ],
        compiler_params=pltpu.CompilerParams(
            collective_id=0, has_side_effects=True, vmem_limit_bytes=60 * 1024 * 1024
        ),
        cost_estimate=pl.CostEstimate(
            flops=20_000_000_000, bytes_accessed=8_000_000, transcendentals=0
        ),
    )(og, hidden, gates, ids, weight)


def shards(out_grad, hidden, gates, expert_ids, down_weight):
    hidden_grad, gate_grad, weight_grad = fused(
        out_grad,
        hidden.reshape(SLOTS, UNITS),
        gates.T,
        expert_ids.T,
        down_weight,
    )
    return weight_grad, hidden_grad.reshape(TOK, 8, UNITS), gate_grad.T


def solution(mesh):
    placed = (
        P("blk", "hid"),
        P("blk", None, "hid"),
        P("blk", None),
        P("blk", None),
        P("blk", "hid", None),
    )
    return jax.shard_map(
        shards,
        mesh=mesh,
        in_specs=placed,
        out_specs=(P("blk", "hid", None), P("blk", None, "hid"), P("blk", None)),
        check_vma=False,
    )
```

```python
import jax
import jax.numpy as jnp
from jax import lax
from jax.experimental import pallas as pl
from jax.experimental.pallas import tpu as pltpu
from jax.sharding import PartitionSpec as P

MESH = pl.DeviceIdType.MESH
BF = jnp.bfloat16
F32 = jnp.float32
NX, NY, NZ, NC = 4, 8, 8, 2
QUAD = 4
CAP = 12
GRP = QUAD * CAP
TOK = 128
LANE = 128
CHUNK = QUAD * TOK
CHUNK_ROWS = CHUNK + 4 * 8
COL = NY * GRP
NQ = NY * QUAD
UNITS = 384
FEATS = 2048
SLOTS = 1024


def dot(a, b):
    return jnp.dot(a, b, preferred_element_type=F32)


def dot_nt(a, b):
    return lax.dot_general(a, b, (((1,), (1,)), ((), ())), preferred_element_type=F32)


def dot_tn(a, b):
    return lax.dot_general(a, b, (((0,), (0,)), ((), ())), preferred_element_type=F32)


def thirds(value):
    high = value.astype(BF)
    rest = value - high.astype(F32)
    middle = rest.astype(BF)
    return high, middle, (rest - middle.astype(F32)).astype(BF)


def kernel(
    og, hidden, gates, ids, weight,
    hidden_grad, gate_out, weight_grad,
    weighted, slot_target, slot_gate, stage, ex, cols, gsel, sendx, rows,
    hs, hx, hq_send, hq, hrows,
    rq_send, rq, r2, rx, undo, w_vmem, wg_vmem, gate_row, gate_recv,
    ex_s, ex_r, ra_s, ra_r, rb_s, rb_r, x_s, x_r,
    hx_s, hx_r, hq_s, hq_r, rq_s, rq_r, rx_s, rx_r, gt_s, gt_r, w_sem, o_sem,
):
    blk = lax.axis_index("blk")
    hid = lax.axis_index("hid")
    x = blk // 32
    y = (blk // 4) % 8
    zhi = (blk // 2) % 2
    core = blk % 2
    z = zhi * 4 + hid
    quad = zhi * 2 + core
    q = blk % 32

    def dev(x_, y_, z_, c_):
        return (x_ * 32 + y_ * 4 + (z_ // 4) * 2 + c_, z_ % 4)

    def dev_q(q_):
        return (x * 32 + q_, hid)

    def remote(src, dst, send_sem, recv_sem, device):
        copy = pltpu.make_async_remote_copy(
            src_ref=src, dst_ref=dst, send_sem=send_sem, recv_sem=recv_sem,
            device_id=device, device_id_type=MESH,
        )
        copy.start()

    def wait_for(ref, sem):
        pltpu.make_async_copy(ref, ref, sem).wait()

    pa = core * y + (1 - core) * z
    pb = core * z + (1 - core) * y

    def dev_ab(a, b):
        return dev(x, core * a + (1 - core) * b, core * b + (1 - core) * a, core)

    barrier = pltpu.get_barrier_semaphore()
    friends = [dev_ab((pa + step) % 8, pb) for step in (1, 7)]
    friends += [dev_ab(pa, (pb + step) % 8) for step in (1, 7)]
    friends += [
        dev((x + d // 2) % 4, y, z, (core + d % 2) % 2) for d in range(1, 8)
    ]
    friends += [dev(x, y, (z + 4) % 8, c) for c in range(2)]
    for friend in friends:
        pl.semaphore_signal(barrier, inc=1, device_id=friend, device_id_type=MESH)

    def feature_block(c, z_):
        return (z_ % 4) * 512 + (z_ // 4) * 256 + c * 128

    for c in range(2):
        for z_ in range(8):
            pltpu.make_async_copy(
                weight.at[0, :, pl.ds(feature_block(c, z_), LANE)],
                w_vmem.at[:, pl.ds((c * 8 + z_) * LANE, LANE)],
                w_sem,
            ).start()

    lane = lax.broadcasted_iota(jnp.int32, (TOK, LANE), 1)
    own_ids = ids[...].astype(F32)
    both = jnp.concatenate(
        [own_ids, gates[...], jnp.zeros((TOK - 16, LANE), F32)], axis=0
    ).T
    id_lanes = jnp.where(lane < 8, both, 0.0)
    gate_lanes = jnp.zeros((TOK, LANE), F32)
    named = jnp.zeros((TOK, LANE), F32)
    for k in range(8):
        gate_lanes = jnp.where(lane % 8 == k, both[:, 8 + k:9 + k], gate_lanes)
        named = named + jnp.where(lane.astype(F32) == both[:, k:k + 1], 1.0, 0.0)
    ids16 = jnp.concatenate([own_ids, jnp.zeros((8, TOK), F32)], axis=0).astype(BF)
    for j in range(QUAD):
        stage[j, 0:TOK, :] = og[:, j * LANE:(j + 1) * LANE]
        stage[j, TOK:TOK + 16, :] = ids16

    high, middle, low = (part.astype(F32) for part in thirds(gate_lanes))
    mixed = jnp.where(
        lane < 8, high,
        jnp.where(lane < 16, middle, jnp.where(lane < 24, low, 0.0)),
    )
    earlier = jnp.where(
        lax.broadcasted_iota(jnp.int32, (TOK, TOK), 1)
        < lax.broadcasted_iota(jnp.int32, (TOK, TOK), 0), 1.0, 0.0,
    ).astype(BF)
    count = dot(earlier, named.astype(BF)).astype(BF)
    slot = lax.broadcasted_iota(jnp.int32, (SLOTS, LANE), 0)
    slot_lane = lax.broadcasted_iota(jnp.int32, (SLOTS, LANE), 1)
    token_of = jnp.where(slot // 8 == slot_lane, 1.0, 0.0).astype(BF)
    turn = slot % 8 == slot_lane % 8
    slot_gate[...] = jnp.broadcast_to(
        jnp.sum(
            jnp.where(turn, dot(token_of, mixed.astype(BF)), 0.0), axis=1, keepdims=True
        ),
        (SLOTS, LANE),
    )
    slot_id = jnp.sum(
        jnp.where(turn, dot(token_of, id_lanes.astype(BF)), 0.0), axis=1, keepdims=True
    )
    slot_rank = jnp.sum(
        jnp.where(slot_lane.astype(F32) == slot_id, dot(token_of, count), 0.0),
        axis=1, keepdims=True,
    )
    slot_target[...] = jnp.broadcast_to(slot_id * float(CAP) + slot_rank, (SLOTS, LANE))
    both = jnp.where(
        slot_lane == 0, slot_id, jnp.where(slot_lane == 1, slot_rank, 0.0)
    ).astype(BF)
    lane16 = lax.broadcasted_iota(jnp.int32, (16, LANE), 1)
    tgt_row = dot_nt(
        jnp.where(lane16 == 0, float(CAP), jnp.where(lane16 == 1, 1.0, 0.0)).astype(BF),
        both,
    )[0:1]
    def select_hidden(dx):
        xd = (x + dx) % 4
        at = lax.broadcasted_iota(jnp.int32, (COL, SLOTS), 0) + xd * COL
        pick = jnp.where(at.astype(F32) == tgt_row, 1.0, 0.0).astype(BF)
        picked = dot(pick, weighted[...]).astype(BF)
        if dx == 0:
            hx[x] = picked
        else:
            hs[dx] = picked

    def send_hidden_x(dx):
        remote(
            hs.at[dx], hx.at[x], hx_s, hx_r.at[dx], dev((x + dx) % 4, y, z, core)
        )

    pl.semaphore_wait(barrier, len(friends))

    for d in range(1, 4):
        other = (quad + d) % 4
        remote(
            stage.at[other], ex.at[quad], ex_s, ex_r.at[d],
            dev(x, y, (other // 2) * 4 + hid, other % 2),
        )
    ex[quad] = stage[quad]

    for i in range(4):
        part = slice(i * 256, (i + 1) * 256)
        for j in range(3):
            weighted[part, j * LANE:(j + 1) * LANE] = (
                slot_gate[part, :] * hidden[part, j * LANE:(j + 1) * LANE].astype(F32)
            ).astype(BF)
    select_hidden(2)
    send_hidden_x(2)

    for d in range(1, 4):
        wait_for(ex.at[0], ex_r.at[d])
    own = cols.at[pb, pa]
    for j in range(QUAD):
        own[j * TOK:(j + 1) * TOK, :] = ex[j, 0:TOK, :]
    own[CHUNK:CHUNK_ROWS, :] = jnp.concatenate(
        [ex[j, TOK:TOK + 16, :].astype(F32)[0:8] for j in range(QUAD)], axis=0
    ).astype(BF)

    half_rows = CHUNK_ROWS // 2
    for step in range(1, 5):
        for way, sign in ((0, 1), (1, -1)):
            a = (pa - sign * (step - 1)) % 8
            if step > 1:
                wait_for(cols.at[0, 0], ra_r.at[way, step - 1])
            ref = cols.at[pb, a]
            if step == 4:
                ref = cols.at[pb, a, pl.ds(way * half_rows, half_rows)]
            remote(ref, ref, ra_s, ra_r.at[way, step], dev_ab((pa + sign) % 8, pb))
        if step == 1:
            select_hidden(1)
            send_hidden_x(1)
        if step == 2:
            select_hidden(3)
            send_hidden_x(3)
        if step == 3:
            select_hidden(0)
    for way in range(2):
        wait_for(cols.at[0, 0, pl.ds(0, half_rows)], ra_r.at[way, 4])

    def ring_has(step, way, piece):
        return step < 4 or piece // 2 == way

    def ring_wait(step):
        for piece in range(4):
            for way in range(2):
                if ring_has(step, way, piece):
                    wait_for(cols.at[0, pl.ds(0, 2), pl.ds(0, CHUNK)], rb_r.at[way, step, piece])
        wait_for(cols.at[0, 0, pl.ds(CHUNK, 32)], rb_r.at[0, step, 4])

    def ring_send(step):
        for way, sign in ((0, 1), (1, -1)):
            if step > 1:
                wait_for(cols.at[0, 0, pl.ds(CHUNK, 32)], rb_r.at[way, step - 1, 4])
            if step < 4 or way == 0:
                ref = cols.at[(pb - sign * (step - 1)) % 8, 0, pl.ds(CHUNK, 32)]
                remote(
                    ref, ref, rb_s, rb_r.at[way, step, 4], dev_ab(pa, (pb + sign) % 8)
                )
        for piece in range(4):
            for way, sign in ((0, 1), (1, -1)):
                b = (pb - sign * (step - 1)) % 8
                if step > 1:
                    wait_for(
                        cols.at[0, pl.ds(0, 2), pl.ds(0, CHUNK)],
                        rb_r.at[way, step - 1, piece],
                    )
                if ring_has(step, way, piece):
                    ref = cols.at[b, pl.ds(2 * piece, 2), pl.ds(0, CHUNK)]
                    remote(
                        ref, ref, rb_s, rb_r.at[way, step, piece],
                        dev_ab(pa, (pb + sign) % 8),
                    )

    before = jnp.where(
        lax.broadcasted_iota(jnp.int32, (TOK, TOK), 0)
        < lax.broadcasted_iota(jnp.int32, (TOK, TOK), 1), 1.0, 0.0,
    ).astype(BF)
    which = lax.broadcasted_iota(jnp.int32, (8, TOK), 0)
    wanted = (
        ((x + which // 2) % 4) * 32 + y * 4 + zhi * 2 + (core + which % 2) % 2
    ).astype(F32)

    def make_pick(col, a, b):
        ids = cols[b, a, CHUNK:CHUNK_ROWS, :].astype(F32)
        found = []
        for j in range(QUAD):
            hit = jnp.zeros((8, TOK), F32)
            for k in range(8):
                row = ids[j * 8 + k:j * 8 + k + 1, :]
                hit = hit + jnp.where(row == wanted, 1.0, 0.0)
            found.append(hit)
        rank = dot(jnp.concatenate(found, axis=0).astype(BF), before)
        code = jnp.concatenate(
            [
                jnp.where(found[j] > 0.5, rank[j * 8:(j + 1) * 8] + float(CAP * j), -1.0)
                for j in range(QUAD)
            ],
            axis=1,
        )
        at = lax.broadcasted_iota(jnp.int32, (GRP, CHUNK), 0).astype(F32)
        for e in range(8):
            gsel[col, e * GRP:(e + 1) * GRP, :] = jnp.where(
                at == code[e:e + 1, :], 1.0, 0.0
            ).astype(BF)

    def select(b, first):
        @pl.when(core == 0)
        def _():
            make_pick(b, 0, b)

        if first:
            @pl.when(core == 1)
            def _():
                def one(a, c):
                    make_pick(a, a, b)
                    return c

                lax.fori_loop(0, 8, one, 0)

        def one_chunk(a, c):
            col = core * a + (1 - core) * b
            block = core * b + (1 - core) * a
            out = dot(gsel[col], cols[b, a, 0:CHUNK, :]).astype(BF)
            lanes = pl.multiple_of(block * LANE, LANE)
            rows[
                pl.ds(pl.multiple_of((col * 4 + x) * GRP, GRP), GRP),
                pl.ds(pl.multiple_of(core * (FEATS // 2) + lanes, LANE), LANE),
            ] = out[0:GRP]
            for e in range(1, 8):
                sendx[col, e, :, pl.ds(lanes, LANE)] = out[e * GRP:(e + 1) * GRP]
            return c

        lax.fori_loop(0, 8, one_chunk, 0)

        @pl.when(core == 0)
        def _():
            send_column(b)

    def send_column(col):
        place = pl.ds(pl.multiple_of((col * 4 + x) * GRP, GRP), GRP)
        half = pl.ds(pl.multiple_of(core * (FEATS // 2), FEATS // 2), FEATS // 2)
        for e in (4, 5, 2, 3, 6, 7, 1):
            remote(
                sendx.at[col, e], rows.at[place, half], x_s, x_r.at[(col - y) % 8],
                dev((x + e // 2) % 4, y, z, (core + e % 2) % 2),
            )

    def outward(i):
        return (1 - 2 * (i % 2)) * ((i + 1) // 2)

    def relay_hidden(g, c):
        block = jnp.concatenate(
            [hx[xs, pl.ds(pl.multiple_of(g * GRP, GRP), GRP), :] for xs in range(4)],
            axis=0,
        )
        out = dot(swap, block).astype(BF)
        for j in range(4):
            hq_send[g * 4 + j] = out[j * GRP:(j + 1) * GRP]
        return c

    def send_hidden(d, c):
        qd = (q + d) % 32
        remote(hq_send.at[qd], hq.at[q], hq_s, hq_r, dev_q(qd))
        return c

    def make_undo(i, c):
        place = pl.ds(pl.multiple_of(i * 128, 128), 128)
        for j in range(NX * COL // LANE):
            at = lax.broadcasted_iota(jnp.int32, (128, LANE), 1) + j * LANE
            undo[place, j * LANE:(j + 1) * LANE] = jnp.where(
                at.astype(F32) == slot_target[place, :], 1.0, 0.0
            ).astype(BF)
        return c

    out_row = lax.broadcasted_iota(jnp.int32, (4 * GRP, 4 * GRP), 0)
    outer = sum(jnp.where(out_row >= n * GRP, 1, 0) for n in range(1, 4))
    within = out_row - outer * GRP
    inner = sum(jnp.where(within >= n * CAP, 1, 0) for n in range(1, 4))
    from_row = inner * GRP + outer * CAP + within - inner * CAP
    in_row = lax.broadcasted_iota(jnp.int32, (4 * GRP, 4 * GRP), 1)
    swap = jnp.where(in_row == from_row, 1.0, 0.0).astype(BF)

    ring_send(1)
    select(pb, True)
    ring_send(2)
    select((pb - 1) % 8, False)
    select((pb + 1) % 8, False)
    ring_send(3)
    select((pb - 2) % 8, False)
    select((pb + 2) % 8, False)
    for dx in range(1, 4):
        wait_for(hx.at[0], hx_r.at[dx])
    lax.fori_loop(0, 8, relay_hidden, 0)
    hq[q] = hq_send[q]
    ring_send(4)
    select((pb - 3) % 8, False)
    select((pb + 3) % 8, False)
    ring_wait(4)
    select((pb + 4) % 8, False)

    @pl.when(core == 1)
    def _():
        send_column(y)
        send_column((y + outward(1)) % 8)

    lax.fori_loop(1, 32, send_hidden, 0)
    lax.fori_loop(0, 8, make_undo, 0)
    wait_for(w_vmem, w_sem)

    def one_column(i):
        ys = (y + outward(i)) % 8
        wait_for(sendx.at[0, pl.ds(1, 7)], x_r.at[outward(i) % 8])

        @pl.when((core == 1) & (i < 6))
        def _():
            send_column((y + outward(i + 2)) % 8)

        block = rows[pl.ds(pl.multiple_of(ys * 4 * GRP, GRP), 4 * GRP), :]
        pre = dot_nt(block, w_vmem[...]).astype(BF)
        out = dot(swap, pre).astype(BF)
        for j in range(4):
            rq_send[ys * 4 + j] = out[j * GRP:(j + 1) * GRP]
        for j in range(4):
            qd = ys * 4 + j

            @pl.when(qd != q)
            def _():
                remote(
                    rq_send.at[qd], rq.at[q], rq_s, rq_r.at[(ys - y) % 8], dev_q(qd)
                )

            @pl.when(qd == q)
            def _():
                rq[q] = rq_send[qd]

    def relay_back(i):
        dy = outward(i) % 8
        g = (y - outward(i)) % 8

        @pl.when(dy == 0)
        def _():
            wait_for(rq.at[pl.ds(0, 3)], rq_r.at[dy])

        @pl.when(dy != 0)
        def _():
            wait_for(rq.at[pl.ds(0, 4)], rq_r.at[dy])

        block = jnp.concatenate([rq[g * 4 + j] for j in range(4)], axis=0)
        out = dot(swap, block).astype(BF)
        place = pl.ds(pl.multiple_of(g * GRP, GRP), GRP)
        for xs in range(4):
            r2[xs, place, :] = out[xs * GRP:(xs + 1) * GRP]
        rx[x, place, :] = r2[x, place, :]
        for dx in (2, 1, 3):
            xd = (x + dx) % 4
            remote(
                r2.at[xd, place], rx.at[x, place], rx_s, rx_r.at[dx],
                dev(xd, y, z, core),
            )

    def column_and_relay(i, c):
        one_column(i)

        @pl.when(i >= 2)
        def _():
            relay_back(i - 2)

        return c

    lax.fori_loop(0, 8, column_and_relay, 0)

    def order_hidden(g, c):
        block = jnp.concatenate([hq[g * 4 + j] for j in range(4)], axis=0)
        hrows[pl.ds(pl.multiple_of(g * 4 * GRP, GRP), 4 * GRP), :] = dot(
            swap, block
        ).astype(BF)
        return c

    def weight_part(c):
        for half in range(4):
            lanes = (c * 8 + half * 2) * LANE
            wg_vmem[:, lanes:lanes + 256] = dot_tn(
                hrows[...], rows[:, lanes:lanes + 256]
            ).astype(BF)
            for z_ in (half * 2, half * 2 + 1):
                pltpu.make_async_copy(
                    wg_vmem.at[:, pl.ds((c * 8 + z_) * LANE, LANE)],
                    weight_grad.at[0, :, pl.ds(feature_block(c, z_), LANE)],
                    o_sem,
                ).start()

    relay_back(6)
    wait_for(hq.at[pl.ds(0, 31)], hq_r)
    lax.fori_loop(0, 8, order_hidden, 0)
    relay_back(7)
    weight_part(0)

    for dx in range(1, 4):
        wait_for(rx.at[0], rx_r.at[dx])
    ones = jnp.ones((8, LANE), BF)

    def take(i, c):
        place = pl.ds(pl.multiple_of(i * 256, 256), 256)
        grads = dot(undo[place, :], rx[...].reshape(NX * COL, UNITS))
        for j in range(3):
            part = slice(j * LANE, (j + 1) * LANE)
            hidden_grad[place, part] = (slot_gate[place, :] * grads[:, part]).astype(BF)
        product = hidden[place, :].astype(F32) * grads
        total = product[:, 0:128] + product[:, 128:256] + product[:, 256:384]
        gate_row[:, place] = sum(dot_nt(ones, part) for part in thirds(total))
        return c

    lax.fori_loop(0, 4, take, 0)
    in_turn = (
        lax.broadcasted_iota(jnp.int32, (8, SLOTS), 1) % 8
        == lax.broadcasted_iota(jnp.int32, (8, SLOTS), 0)
    )
    token_of = jnp.where(slot // 8 == slot_lane, 1.0, 0.0).astype(BF)
    gate_recv[hid] = sum(
        dot(part, token_of) for part in thirds(jnp.where(in_turn, gate_row[...], 0.0))
    )

    for d in range(1, 4):
        remote(
            gate_recv.at[hid], gate_recv.at[hid], gt_s, gt_r.at[d],
            (blk, (hid + d) % 4),
        )
    weight_part(1)
    for d in range(1, 4):
        wait_for(gate_recv.at[0], gt_r.at[d])
    gate_out[...] = (gate_recv[0] + gate_recv[1]) + (gate_recv[2] + gate_recv[3])

    wait_for(stage.at[pl.ds(0, 3)], ex_s)
    wait_for(cols.at[0, pl.ds(0, 7)], ra_s)
    wait_for(cols.at[pl.ds(0, 7), :, pl.ds(0, CHUNK)], rb_s)
    wait_for(cols.at[0, pl.ds(0, 7), pl.ds(CHUNK, 32)], rb_s)
    wait_for(sendx.at[:, pl.ds(1, 7)], x_s)
    wait_for(hs.at[pl.ds(1, 3)], hx_s)
    wait_for(hq_send.at[pl.ds(0, 31)], hq_s)
    wait_for(rq_send.at[pl.ds(0, 31)], rq_s)
    wait_for(r2.at[pl.ds(0, 3)], rx_s)
    wait_for(gate_recv.at[pl.ds(0, 3)], gt_s)
    wait_for(wg_vmem, o_sem)


def fused(og, hidden, gates, ids, weight):
    vmem = pl.BlockSpec(memory_space=pltpu.VMEM)
    hbm = pl.BlockSpec(memory_space=pl.ANY)
    dma = pltpu.SemaphoreType.DMA
    buf = lambda *shape: pltpu.VMEM(shape, BF)
    return pl.pallas_call(
        kernel,
        out_shape=(
            jax.ShapeDtypeStruct((SLOTS, UNITS), BF),
            jax.ShapeDtypeStruct((8, TOK), F32),
            jax.ShapeDtypeStruct((1, UNITS, FEATS), BF),
        ),
        in_specs=[vmem] * 4 + [hbm],
        out_specs=(vmem, vmem, hbm),
        scratch_shapes=[
            buf(SLOTS, UNITS),
            pltpu.VMEM((SLOTS, LANE), F32),
            pltpu.VMEM((SLOTS, LANE), F32),
            buf(QUAD, TOK + 16, LANE),
            buf(QUAD, TOK + 16, LANE),
            buf(8, 8, CHUNK_ROWS, LANE),
            buf(8, 8 * GRP, CHUNK),
            buf(8, 8, GRP, FEATS // 2),
            buf(NX * COL, FEATS),
            buf(NX, COL, UNITS),
            buf(NX, COL, UNITS),
            buf(NQ, GRP, UNITS),
            buf(NQ, GRP, UNITS),
            buf(NX * COL, UNITS),
            buf(NQ, GRP, UNITS),
            buf(NQ, GRP, UNITS),
            buf(NX, COL, UNITS),
            buf(NX, COL, UNITS),
            buf(SLOTS, NX * COL),
            buf(UNITS, FEATS),
            buf(UNITS, FEATS),
            pltpu.VMEM((8, SLOTS), F32),
            pltpu.VMEM((4, 8, TOK), F32),
            dma, dma((4,)),
            dma, dma((2, 5)),
            dma, dma((2, 5, 5)),
            dma, dma((8,)),
            dma, dma((4,)),
            dma, dma,
            dma, dma((8,)),
            dma, dma((4,)),
            dma, dma((4,)),
            dma, dma,
        ],
        compiler_params=pltpu.CompilerParams(
            collective_id=0, has_side_effects=True, vmem_limit_bytes=60 * 1024 * 1024
        ),
        cost_estimate=pl.CostEstimate(
            flops=20_000_000_000, bytes_accessed=8_000_000, transcendentals=0
        ),
    )(og, hidden, gates, ids, weight)


def shards(out_grad, hidden, gates, expert_ids, down_weight):
    hidden_grad, gate_grad, weight_grad = fused(
        out_grad,
        hidden.reshape(SLOTS, UNITS),
        gates.T,
        expert_ids.T,
        down_weight,
    )
    return weight_grad, hidden_grad.reshape(TOK, 8, UNITS), gate_grad.T


def solution(mesh):
    placed = (
        P("blk", "hid"),
        P("blk", None, "hid"),
        P("blk", None),
        P("blk", None),
        P("blk", "hid", None),
    )
    return jax.shard_map(
        shards,
        mesh=mesh,
        in_specs=placed,
        out_specs=(P("blk", "hid", None), P("blk", None, "hid"), P("blk", None)),
        check_vma=False,
    )
```

```python
import jax
import jax.numpy as jnp
from jax import lax
from jax.experimental import pallas as pl
from jax.experimental.pallas import tpu as pltpu
from jax.sharding import PartitionSpec as P

MESH = pl.DeviceIdType.MESH
BF = jnp.bfloat16
F32 = jnp.float32
NX, NY, NZ, NC = 4, 8, 8, 2
QUAD = 4
CAP = 12
GRP = QUAD * CAP
TOK = 128
LANE = 128
CHUNK = QUAD * TOK
CHUNK_ROWS = CHUNK + 4 * 8
COL = NY * GRP
NQ = NY * QUAD
UNITS = 384
FEATS = 2048
SLOTS = 1024


def dot(a, b):
    return jnp.dot(a, b, preferred_element_type=F32)


def dot_nt(a, b):
    return lax.dot_general(a, b, (((1,), (1,)), ((), ())), preferred_element_type=F32)


def dot_tn(a, b):
    return lax.dot_general(a, b, (((0,), (0,)), ((), ())), preferred_element_type=F32)


def thirds(value):
    high = value.astype(BF)
    rest = value - high.astype(F32)
    middle = rest.astype(BF)
    return high, middle, (rest - middle.astype(F32)).astype(BF)


def kernel(
    og, hidden, gates, ids, weight,
    hidden_grad, gate_out, weight_grad,
    weighted, slot_target, slot_gate, stage, ex, cols, gsel, sendx, recvx, rows,
    hs, hx, hq_send, hq, pre_rows, hrows,
    rq_send, rq, r2, rx, undo, w_vmem, wg_vmem, gate_row, gate_recv,
    ex_s, ex_r, ra_s, ra_r, rb_s, rb_r, x_s, x_r,
    hx_s, hx_r, hq_s, hq_r, rq_s, rq_r, rx_s, rx_r, gt_s, gt_r, w_sem, o_sem,
):
    blk = lax.axis_index("blk")
    hid = lax.axis_index("hid")
    x = blk // 32
    y = (blk // 4) % 8
    zhi = (blk // 2) % 2
    core = blk % 2
    z = zhi * 4 + hid
    quad = zhi * 2 + core
    q = blk % 32

    def dev(x_, y_, z_, c_):
        return (x_ * 32 + y_ * 4 + (z_ // 4) * 2 + c_, z_ % 4)

    def dev_q(q_):
        return (x * 32 + q_, hid)

    def remote(src, dst, send_sem, recv_sem, device):
        copy = pltpu.make_async_remote_copy(
            src_ref=src, dst_ref=dst, send_sem=send_sem, recv_sem=recv_sem,
            device_id=device, device_id_type=MESH,
        )
        copy.start()

    def wait_for(ref, sem):
        pltpu.make_async_copy(ref, ref, sem).wait()

    pa = core * y + (1 - core) * z
    pb = core * z + (1 - core) * y

    def dev_ab(a, b):
        return dev(x, core * a + (1 - core) * b, core * b + (1 - core) * a, core)

    barrier = pltpu.get_barrier_semaphore()
    friends = [dev_ab((pa + step) % 8, pb) for step in (1, 7)]
    friends += [dev_ab(pa, (pb + step) % 8) for step in (1, 7)]
    friends += [
        dev((x + d // 2) % 4, y, z, (core + d % 2) % 2) for d in range(1, 8)
    ]
    friends += [dev(x, y, (z + 4) % 8, c) for c in range(2)]
    for friend in friends:
        pl.semaphore_signal(barrier, inc=1, device_id=friend, device_id_type=MESH)

    def feature_block(c, z_):
        return (z_ % 4) * 512 + (z_ // 4) * 256 + c * 128

    for c in range(2):
        for z_ in range(8):
            pltpu.make_async_copy(
                weight.at[0, :, pl.ds(feature_block(c, z_), LANE)],
                w_vmem.at[:, pl.ds((c * 8 + z_) * LANE, LANE)],
                w_sem,
            ).start()

    lane = lax.broadcasted_iota(jnp.int32, (TOK, LANE), 1)
    own_ids = ids[...].astype(F32)
    both = jnp.concatenate(
        [own_ids, gates[...], jnp.zeros((TOK - 16, LANE), F32)], axis=0
    ).T
    id_lanes = jnp.where(lane < 8, both, 0.0)
    gate_lanes = jnp.zeros((TOK, LANE), F32)
    named = jnp.zeros((TOK, LANE), F32)
    for k in range(8):
        gate_lanes = jnp.where(lane % 8 == k, both[:, 8 + k:9 + k], gate_lanes)
        named = named + jnp.where(lane.astype(F32) == both[:, k:k + 1], 1.0, 0.0)
    ids16 = jnp.concatenate([own_ids, jnp.zeros((8, TOK), F32)], axis=0).astype(BF)
    for j in range(QUAD):
        stage[j, 0:TOK, :] = og[:, j * LANE:(j + 1) * LANE]
        stage[j, TOK:TOK + 16, :] = ids16

    pl.semaphore_wait(barrier, len(friends))

    for d in range(1, 4):
        other = (quad + d) % 4
        remote(
            stage.at[other], ex.at[quad], ex_s, ex_r.at[d],
            dev(x, y, (other // 2) * 4 + hid, other % 2),
        )
    ex[quad] = stage[quad]

    high, middle, low = (part.astype(F32) for part in thirds(gate_lanes))
    mixed = jnp.where(
        lane < 8, high,
        jnp.where(lane < 16, middle, jnp.where(lane < 24, low, 0.0)),
    )
    earlier = jnp.where(
        lax.broadcasted_iota(jnp.int32, (TOK, TOK), 1)
        < lax.broadcasted_iota(jnp.int32, (TOK, TOK), 0), 1.0, 0.0,
    ).astype(BF)
    count = dot(earlier, named.astype(BF)).astype(BF)
    slot = lax.broadcasted_iota(jnp.int32, (SLOTS, LANE), 0)
    slot_lane = lax.broadcasted_iota(jnp.int32, (SLOTS, LANE), 1)
    token_of = jnp.where(slot // 8 == slot_lane, 1.0, 0.0).astype(BF)
    turn = slot % 8 == slot_lane % 8
    slot_gate[...] = jnp.broadcast_to(
        jnp.sum(
            jnp.where(turn, dot(token_of, mixed.astype(BF)), 0.0), axis=1, keepdims=True
        ),
        (SLOTS, LANE),
    )
    slot_id = jnp.sum(
        jnp.where(turn, dot(token_of, id_lanes.astype(BF)), 0.0), axis=1, keepdims=True
    )
    slot_rank = jnp.sum(
        jnp.where(slot_lane.astype(F32) == slot_id, dot(token_of, count), 0.0),
        axis=1, keepdims=True,
    )
    slot_target[...] = jnp.broadcast_to(slot_id * float(CAP) + slot_rank, (SLOTS, LANE))
    both = jnp.where(
        slot_lane == 0, slot_id, jnp.where(slot_lane == 1, slot_rank, 0.0)
    ).astype(BF)
    lane16 = lax.broadcasted_iota(jnp.int32, (16, LANE), 1)
    tgt_row = dot_nt(
        jnp.where(lane16 == 0, float(CAP), jnp.where(lane16 == 1, 1.0, 0.0)).astype(BF),
        both,
    )[0:1]
    for i in range(4):
        part = slice(i * 256, (i + 1) * 256)
        for j in range(3):
            weighted[part, j * LANE:(j + 1) * LANE] = (
                slot_gate[part, :] * hidden[part, j * LANE:(j + 1) * LANE].astype(F32)
            ).astype(BF)

    def select_hidden(dx):
        xd = (x + dx) % 4
        at = lax.broadcasted_iota(jnp.int32, (COL, SLOTS), 0) + xd * COL
        pick = jnp.where(at.astype(F32) == tgt_row, 1.0, 0.0).astype(BF)
        picked = dot(pick, weighted[...]).astype(BF)
        if dx == 0:
            hx[x] = picked
        else:
            hs[dx] = picked

    def send_hidden_x(dx):
        remote(
            hs.at[dx], hx.at[x], hx_s, hx_r.at[dx], dev((x + dx) % 4, y, z, core)
        )

    select_hidden(2)

    send_hidden_x(2)

    for d in range(1, 4):
        wait_for(ex.at[0], ex_r.at[d])
    own = cols.at[pb, pa]
    for j in range(QUAD):
        own[j * TOK:(j + 1) * TOK, :] = ex[j, 0:TOK, :]
    own[CHUNK:CHUNK_ROWS, :] = jnp.concatenate(
        [ex[j, TOK:TOK + 16, :].astype(F32)[0:8] for j in range(QUAD)], axis=0
    ).astype(BF)

    half_rows = CHUNK_ROWS // 2
    for step in range(1, 5):
        for way, sign in ((0, 1), (1, -1)):
            a = (pa - sign * (step - 1)) % 8
            if step > 1:
                wait_for(cols.at[0, 0], ra_r.at[way, step - 1])
            ref = cols.at[pb, a]
            if step == 4:
                ref = cols.at[pb, a, pl.ds(way * half_rows, half_rows)]
            remote(ref, ref, ra_s, ra_r.at[way, step], dev_ab((pa + sign) % 8, pb))
        if step == 1:
            select_hidden(1)
            send_hidden_x(1)
        if step == 2:
            select_hidden(3)
            send_hidden_x(3)
        if step == 3:
            select_hidden(0)
    for way in range(2):
        wait_for(cols.at[0, 0, pl.ds(0, half_rows)], ra_r.at[way, 4])

    def ring_has(step, way, piece):
        return step < 4 or piece // 2 == way

    def ring_wait(step):
        for piece in range(4):
            for way in range(2):
                if ring_has(step, way, piece):
                    wait_for(cols.at[0, pl.ds(0, 2)], rb_r.at[way, step, piece])

    def ring_send(step):
        for piece in range(4):
            for way, sign in ((0, 1), (1, -1)):
                b = (pb - sign * (step - 1)) % 8
                if step > 1:
                    wait_for(cols.at[0, pl.ds(0, 2)], rb_r.at[way, step - 1, piece])
                if ring_has(step, way, piece):
                    ref = cols.at[b, pl.ds(2 * piece, 2)]
                    remote(
                        ref, ref, rb_s, rb_r.at[way, step, piece],
                        dev_ab(pa, (pb + sign) % 8),
                    )

    before = jnp.where(
        lax.broadcasted_iota(jnp.int32, (TOK, TOK), 0)
        < lax.broadcasted_iota(jnp.int32, (TOK, TOK), 1), 1.0, 0.0,
    ).astype(BF)
    which = lax.broadcasted_iota(jnp.int32, (8, TOK), 0)
    wanted = (
        ((x + which // 2) % 4) * 32 + y * 4 + zhi * 2 + (core + which % 2) % 2
    ).astype(F32)

    def make_pick(col, a, b):
        ids = cols[b, a, CHUNK:CHUNK_ROWS, :].astype(F32)
        found = []
        for j in range(QUAD):
            hit = jnp.zeros((8, TOK), F32)
            for k in range(8):
                row = ids[j * 8 + k:j * 8 + k + 1, :]
                hit = hit + jnp.where(row == wanted, 1.0, 0.0)
            found.append(hit)
        rank = dot(jnp.concatenate(found, axis=0).astype(BF), before)
        code = jnp.concatenate(
            [
                jnp.where(found[j] > 0.5, rank[j * 8:(j + 1) * 8] + float(CAP * j), -1.0)
                for j in range(QUAD)
            ],
            axis=1,
        )
        at = lax.broadcasted_iota(jnp.int32, (GRP, CHUNK), 0).astype(F32)
        for e in range(8):
            gsel[col, e * GRP:(e + 1) * GRP, :] = jnp.where(
                at == code[e:e + 1, :], 1.0, 0.0
            ).astype(BF)

    def select(b, first):
        @pl.when(core == 0)
        def _():
            make_pick(b, 0, b)

        if first:
            @pl.when(core == 1)
            def _():
                def one(a, c):
                    make_pick(a, a, b)
                    return c

                lax.fori_loop(0, 8, one, 0)

        def one_chunk(a, c):
            col = core * a + (1 - core) * b
            out = dot(gsel[col], cols[b, a, 0:CHUNK, :]).astype(BF)
            place = pl.ds(pl.multiple_of(a * GRP, GRP), GRP)
            recvx[core, x, b, place, :] = out[0:GRP]
            for e in range(1, 8):
                sendx[b, e, place, :] = out[e * GRP:(e + 1) * GRP]
            return c

        lax.fori_loop(0, 8, one_chunk, 0)
        for e in (4, 5, 2, 3, 6, 7, 1):
            remote(
                sendx.at[b, e], recvx.at[core, x, b], x_s, x_r.at[e // 2],
                dev((x + e // 2) % 4, y, z, (core + e % 2) % 2),
            )

    ring_send(1)
    select(pb, True)
    ring_send(2)
    select((pb - 1) % 8, False)
    select((pb + 1) % 8, False)

    ring_send(3)
    select((pb - 2) % 8, False)
    select((pb + 2) % 8, False)
    ring_send(4)
    select((pb - 3) % 8, False)
    select((pb + 3) % 8, False)

    for dx in range(1, 4):
        wait_for(hx.at[0], hx_r.at[dx])
    out_row = lax.broadcasted_iota(jnp.int32, (4 * GRP, 4 * GRP), 0)
    outer = sum(jnp.where(out_row >= n * GRP, 1, 0) for n in range(1, 4))
    within = out_row - outer * GRP
    inner = sum(jnp.where(within >= n * CAP, 1, 0) for n in range(1, 4))
    from_row = inner * GRP + outer * CAP + within - inner * CAP
    in_row = lax.broadcasted_iota(jnp.int32, (4 * GRP, 4 * GRP), 1)
    swap = jnp.where(in_row == from_row, 1.0, 0.0).astype(BF)

    def relay_hidden(g, c):
        block = jnp.concatenate(
            [hx[xs, pl.ds(pl.multiple_of(g * GRP, GRP), GRP), :] for xs in range(4)],
            axis=0,
        )
        out = dot(swap, block).astype(BF)
        for j in range(4):
            hq_send[g * 4 + j] = out[j * GRP:(j + 1) * GRP]
        return c

    lax.fori_loop(0, 8, relay_hidden, 0)
    hq[q] = hq_send[q]


    ring_wait(4)

    def send_hidden(d, c):
        qd = (q + d) % 32
        remote(hq_send.at[qd], hq.at[q], hq_s, hq_r, dev_q(qd))
        return c

    lax.fori_loop(1, 32, send_hidden, 0)

    select((pb + 4) % 8, False)

    wait_for(w_vmem, w_sem)
    for dx in (0, 1, 3, 2):
        xs = (x - dx) % 4
        if dx == 0:
            wait_for(recvx.at[0, 0], x_r.at[0])
        else:
            wait_for(recvx.at[:, 0], x_r.at[dx])
        place = pl.ds(pl.multiple_of(xs * COL, COL), COL)
        for a in range(8):
            rows[place, a * LANE:(a + 1) * LANE] = recvx[
                0, xs, :, a * GRP:(a + 1) * GRP, :
            ].reshape(COL, LANE)
            rows[place, FEATS // 2 + a * LANE:FEATS // 2 + (a + 1) * LANE] = recvx[
                1, xs, a
            ]
        pre_rows[place, :] = dot_nt(rows[place, :], w_vmem[...]).astype(BF)

    def away(i):
        first = 1 - i % 2 * 2 + (i // 2) * 2 * (1 - i % 2 * 2)
        second = (i % 2) * 4 + ((i - 4) // 2) * 2
        return jnp.where(i < 4, first, second) % 8

    def return_group(i, c):
        ys = (y + away(i)) % 8
        block = jnp.concatenate(
            [
                pre_rows[pl.ds(pl.multiple_of(xs * COL + ys * GRP, GRP), GRP), :]
                for xs in range(4)
            ],
            axis=0,
        )
        out = dot(swap, block).astype(BF)
        for j in range(4):
            rq_send[ys * 4 + j] = out[j * GRP:(j + 1) * GRP]
        for j in range(4):
            qd = ys * 4 + j

            @pl.when(qd != q)
            def _():
                remote(
                    rq_send.at[qd], rq.at[q], rq_s, rq_r.at[(ys - y) % 8], dev_q(qd)
                )

            @pl.when(qd == q)
            def _():
                rq[q] = rq_send[qd]
        return c

    lax.fori_loop(0, 4, return_group, 0)

    wait_for(hq.at[pl.ds(0, 31)], hq_r)

    def order_hidden(g, c):
        block = jnp.concatenate([hq[g * 4 + j] for j in range(4)], axis=0)
        out = dot(swap, block).astype(BF)
        for xs in range(4):
            hrows[pl.ds(pl.multiple_of(xs * COL + g * GRP, GRP), GRP), :] = out[
                xs * GRP:(xs + 1) * GRP
            ]
        return c

    lax.fori_loop(0, 8, order_hidden, 0)
    for c in range(2):
        for half in range(4):
            lanes = (c * 8 + half * 2) * LANE
            wg_vmem[:, lanes:lanes + 256] = dot_tn(
                hrows[...], rows[:, lanes:lanes + 256]
            ).astype(BF)
            for z_ in (half * 2, half * 2 + 1):
                pltpu.make_async_copy(
                    wg_vmem.at[:, pl.ds((c * 8 + z_) * LANE, LANE)],
                    weight_grad.at[0, :, pl.ds(feature_block(c, z_), LANE)],
                    o_sem,
                ).start()

    lax.fori_loop(4, 8, return_group, 0)

    def relay_back(i, c):
        dy = away(i)
        g = (y - dy) % 8

        @pl.when(dy == 0)
        def _():
            wait_for(rq.at[pl.ds(0, 3)], rq_r.at[dy])

        @pl.when(dy != 0)
        def _():
            wait_for(rq.at[pl.ds(0, 4)], rq_r.at[dy])

        block = jnp.concatenate([rq[g * 4 + j] for j in range(4)], axis=0)
        out = dot(swap, block).astype(BF)
        place = pl.ds(pl.multiple_of(g * GRP, GRP), GRP)
        for xs in range(4):
            r2[xs, place, :] = out[xs * GRP:(xs + 1) * GRP]
        rx[x, place, :] = r2[x, place, :]
        for dx in (2, 1, 3):
            xd = (x + dx) % 4
            remote(
                r2.at[xd, place], rx.at[x, place], rx_s, rx_r.at[dx],
                dev(xd, y, z, core),
            )
        return c

    lax.fori_loop(0, 8, relay_back, 0)

    def make_undo(i, c):
        place = pl.ds(pl.multiple_of(i * 128, 128), 128)
        for j in range(NX * COL // LANE):
            at = lax.broadcasted_iota(jnp.int32, (128, LANE), 1) + j * LANE
            undo[place, j * LANE:(j + 1) * LANE] = jnp.where(
                at.astype(F32) == slot_target[place, :], 1.0, 0.0
            ).astype(BF)
        return c

    lax.fori_loop(0, 8, make_undo, 0)
    for dx in range(1, 4):
        wait_for(rx.at[0], rx_r.at[dx])
    ones = jnp.ones((8, LANE), BF)

    def take(i, c):
        place = pl.ds(pl.multiple_of(i * 256, 256), 256)
        grads = dot(undo[place, :], rx[...].reshape(NX * COL, UNITS))
        for j in range(3):
            part = slice(j * LANE, (j + 1) * LANE)
            hidden_grad[place, part] = (slot_gate[place, :] * grads[:, part]).astype(BF)
        product = hidden[place, :].astype(F32) * grads
        total = product[:, 0:128] + product[:, 128:256] + product[:, 256:384]
        gate_row[:, place] = sum(dot_nt(ones, part) for part in thirds(total))
        return c

    lax.fori_loop(0, 4, take, 0)
    in_turn = (
        lax.broadcasted_iota(jnp.int32, (8, SLOTS), 1) % 8
        == lax.broadcasted_iota(jnp.int32, (8, SLOTS), 0)
    )
    token_of = jnp.where(slot // 8 == slot_lane, 1.0, 0.0).astype(BF)
    gate_recv[hid] = sum(
        dot(part, token_of) for part in thirds(jnp.where(in_turn, gate_row[...], 0.0))
    )

    for d in range(1, 4):
        remote(
            gate_recv.at[hid], gate_recv.at[hid], gt_s, gt_r.at[d],
            (blk, (hid + d) % 4),
        )
    for d in range(1, 4):
        wait_for(gate_recv.at[0], gt_r.at[d])
    gate_out[...] = (gate_recv[0] + gate_recv[1]) + (gate_recv[2] + gate_recv[3])

    wait_for(stage.at[pl.ds(0, 3)], ex_s)
    wait_for(cols.at[0, pl.ds(0, 7)], ra_s)
    wait_for(cols.at[pl.ds(0, 7)], rb_s)
    wait_for(sendx.at[:, pl.ds(1, 7)], x_s)
    wait_for(hs.at[pl.ds(1, 3)], hx_s)
    wait_for(hq_send.at[pl.ds(0, 31)], hq_s)
    wait_for(rq_send.at[pl.ds(0, 31)], rq_s)
    wait_for(r2.at[pl.ds(0, 3)], rx_s)
    wait_for(gate_recv.at[pl.ds(0, 3)], gt_s)
    wait_for(wg_vmem, o_sem)


def fused(og, hidden, gates, ids, weight):
    vmem = pl.BlockSpec(memory_space=pltpu.VMEM)
    hbm = pl.BlockSpec(memory_space=pl.ANY)
    dma = pltpu.SemaphoreType.DMA
    buf = lambda *shape: pltpu.VMEM(shape, BF)
    return pl.pallas_call(
        kernel,
        out_shape=(
            jax.ShapeDtypeStruct((SLOTS, UNITS), BF),
            jax.ShapeDtypeStruct((8, TOK), F32),
            jax.ShapeDtypeStruct((1, UNITS, FEATS), BF),
        ),
        in_specs=[vmem] * 4 + [hbm],
        out_specs=(vmem, vmem, hbm),
        scratch_shapes=[
            buf(SLOTS, UNITS),
            pltpu.VMEM((SLOTS, LANE), F32),
            pltpu.VMEM((SLOTS, LANE), F32),
            buf(QUAD, TOK + 16, LANE),
            buf(QUAD, TOK + 16, LANE),
            buf(8, 8, CHUNK_ROWS, LANE),
            buf(8, 8 * GRP, CHUNK),
            buf(8, 8, COL, LANE),
            buf(2, NX, 8, COL, LANE),
            buf(NX * COL, FEATS),
            buf(NX, COL, UNITS),
            buf(NX, COL, UNITS),
            buf(NQ, GRP, UNITS),
            buf(NQ, GRP, UNITS),
            buf(NX * COL, UNITS),
            buf(NX * COL, UNITS),
            buf(NQ, GRP, UNITS),
            buf(NQ, GRP, UNITS),
            buf(NX, COL, UNITS),
            buf(NX, COL, UNITS),
            buf(SLOTS, NX * COL),
            buf(UNITS, FEATS),
            buf(UNITS, FEATS),
            pltpu.VMEM((8, SLOTS), F32),
            pltpu.VMEM((4, 8, TOK), F32),
            dma, dma((4,)),
            dma, dma((2, 5)),
            dma, dma((2, 5, 4)),
            dma, dma((4,)),
            dma, dma((4,)),
            dma, dma,
            dma, dma((8,)),
            dma, dma((4,)),
            dma, dma((4,)),
            dma, dma,
        ],
        compiler_params=pltpu.CompilerParams(
            collective_id=0, has_side_effects=True, vmem_limit_bytes=60 * 1024 * 1024
        ),
        cost_estimate=pl.CostEstimate(
            flops=20_000_000_000, bytes_accessed=8_000_000, transcendentals=0
        ),
    )(og, hidden, gates, ids, weight)


def shards(out_grad, hidden, gates, expert_ids, down_weight):
    hidden_grad, gate_grad, weight_grad = fused(
        out_grad,
        hidden.reshape(SLOTS, UNITS),
        gates.T,
        expert_ids.T,
        down_weight,
    )
    return weight_grad, hidden_grad.reshape(TOK, 8, UNITS), gate_grad.T


def solution(mesh):
    placed = (
        P("blk", "hid"),
        P("blk", None, "hid"),
        P("blk", None),
        P("blk", None),
        P("blk", "hid", None),
    )
    return jax.shard_map(
        shards,
        mesh=mesh,
        in_specs=placed,
        out_specs=(P("blk", "hid", None), P("blk", None, "hid"), P("blk", None)),
        check_vma=False,
    )
```
